256 devices in a mesh: harm: 8 (over z_lo, core), prop: 32 (over z_hi, y, x).
Axes of the slice: x: 4, y: 4, z: 8 (z_hi: 2, z_lo: 4; z = z_hi * 4 + z_lo), core: 2. Of those that a mesh axis runs over, the one named last changes fastest.
Arguments:
- rhs_field: float32 [2, 6, 64, 65536], P(None, None, 'harm', 'prop'), may hold values from -48 to 48
- field_guess: float32 [2, 6, 64, 65536], P(None, None, 'harm', 'prop'), may hold values from -6 to 6
- permittivity: float32 [65536], P('prop'), may hold values from 1 to 4
- mod_cells: int32 [32, 640], P('prop'), may hold values from 0 to 2047, as said below
- mod_count: int32 [32], P('prop'), may hold values from 80 to 640
- mod_profile: int32 [32, 640], P('prop'), may hold values from 0 to 15
- mod_amp: float32 [16], replicated, may hold values from 0.25 to 1
- mod_phase: float32 [16], replicated, may hold values from -3.140625 to 3.140625
Outputs:
- fields: float32 [2, 6, 64, 65536], P(None, None, 'harm', 'prop')
The draws below stay inside these ranges and needn't reach their ends.
Inputs may be any that keep to these rules, and one draw needn't show every extreme that they name: `mod_cells`: each slab's list names 640 different cells of that slab.
All inputs are finite; a program needn't handle non-finite values.
Results may differ from the reference program's by a relative error of at most 0.0003.
Values sent between devices are 32-bit elements; how exact they have to be, the bound alone decides.
A program may use at most 256 MiB of HBM per device.

```python
import math
import jax
import jax.numpy as jnp
from jax import lax

HARMONICS = 64
TY = 32
TX = 64
PLANES_DEV = 1
PROFILES = 16
ITERS = 2
SLABS = 32
PLANES = 32
CELLS_DEV = 2048
CELLS = 65536
MOD_CAP = 640


def draw_mod_cells(key, part):
    slab_keys = jax.random.split(key, SLABS)

    def one_slab(slab_key):
        return jax.random.permutation(slab_key, CELLS_DEV)[:MOD_CAP]
    return jax.vmap(one_slab)(slab_keys).astype(jnp.int32)


def draw_mod_count(key, part):
    first_key = jax.random.fold_in(key, 11)
    second_key = jax.random.fold_in(key, 23)
    halvings = jax.random.randint(first_key, (SLABS,), 0, 4)
    counts = MOD_CAP // jnp.left_shift(jnp.ones((SLABS,), jnp.int32), halvings)
    fullest = jax.random.randint(second_key, (), 0, SLABS)
    return counts.at[fullest].set(MOD_CAP).astype(jnp.int32)


def set_ends(array, own_key, low, high):
    longest = array.shape.index(max(array.shape))
    spots = []
    for shift in (0, 1):
        where = [jax.random.randint(jax.random.fold_in(own_key, axis), (), 0, length) for axis, length in enumerate(array.shape)]
        where[longest] = (where[longest] + shift) % array.shape[longest]
        spots.append(tuple(where))
    return array.at[spots[0]].set(low).at[spots[1]].set(high)


def block_scale(stream_key, shape, cuts, least, largest):
    def one(axis_at, shards_of):
        draws = jax.random.uniform(jax.random.fold_in(jax.random.fold_in(stream_key, 6), axis_at), (shards_of,), jnp.float32, least / len(cuts), largest / len(cuts))
        return jnp.repeat(jnp.exp(draws), shape[axis_at] // shards_of).reshape((-1,) + (1,) * (len(shape) - axis_at - 1))

    gain = one(*cuts[0])
    for cut in cuts[1:]:
        gain = gain * one(*cut)
    return gain


def bell_draw(stream_key, shape, width, limit, shards=(), kind=jnp.bfloat16):
    entries = width * jax.random.normal(stream_key, shape, jnp.float32)
    if shards:
        entries = entries * block_scale(stream_key, shape, shards, -0.22, 0.18)
    return jnp.clip(entries, -limit, limit).astype(kind)


def setup_inputs(seed: int = 0) -> dict:
    key_of = jax.random.split(jax.random.key(seed), 9)
    rhs_field = bell_draw(key_of[0], (2, 6, HARMONICS, CELLS), 8.0, 48.0, ((2, 8), (3, 32)), jnp.float32)
    field_guess = bell_draw(key_of[1], (2, 6, HARMONICS, CELLS), 1.0, 6.0, ((2, 8), (3, 32)), jnp.float32)
    permittivity = jnp.clip(jnp.exp(math.log(4.0) - 1.3862944 * jax.random.uniform(key_of[2], (CELLS,), jnp.float32) ** block_scale(key_of[2], (CELLS,), ((0, 32),), -0.2, 0.2)), 1.0, 4.0)
    mod_cells = draw_mod_cells(jax.random.fold_in(key_of[8], 71), 0)
    mod_count = draw_mod_count(jax.random.fold_in(key_of[8], 71), 0)
    mod_profile = set_ends(jax.random.randint(key_of[5], (SLABS, MOD_CAP), 0, PROFILES), jax.random.fold_in(key_of[5], 1), 0, PROFILES - 1).astype(jnp.int32)
    mod_amp = jnp.clip(jnp.exp(jax.random.uniform(key_of[6], (PROFILES,), jnp.float32, math.log(0.25), math.log(1.0))), 0.25, 1.0)
    mod_phase = jnp.clip(jax.random.uniform(key_of[7], (PROFILES,), jnp.float32, -3.140625, 3.140625), -3.140625, 3.140625)
    return dict(rhs_field=rhs_field, field_guess=field_guess, permittivity=permittivity, mod_cells=mod_cells, mod_count=mod_count, mod_profile=mod_profile, mod_amp=mod_amp, mod_phase=mod_phase)


BASE_FREQUENCY = 6.0
MOD_FREQUENCY = 0.05
WAVE_NUMBER = 0.3


def diff_up(field, dim_axis, edge):
    rest = lax.slice_in_dim(field, 1, field.shape[dim_axis], axis=dim_axis)
    return jnp.concatenate([rest, edge], axis=dim_axis) - field


def diff_down(field, dim_axis, edge):
    rest = lax.slice_in_dim(field, 0, field.shape[dim_axis] - 1, axis=dim_axis)
    return field - jnp.concatenate([edge, rest], axis=dim_axis)


def curl_up(field, upper_face):
    def along_y(part):
        return diff_up(part, -2, jnp.zeros_like(part[..., :1, :]))

    def along_x(part):
        return diff_up(part, -1, jnp.zeros_like(part[..., :1]))

    def along_z(part, face):
        return diff_up(part, -3, face[..., None, :, :])

    comp_x, comp_y, comp_z = field[:, 0], field[:, 1], field[:, 2]
    first = along_y(comp_z) - along_z(comp_y, upper_face[:, 1])
    second = along_z(comp_x, upper_face[:, 0]) - along_x(comp_z)
    third = along_x(comp_y) - along_y(comp_x)
    return jnp.stack([first, second, third], axis=1)


def curl_down(field, lower_face):
    def along_y(part):
        return diff_down(part, -2, jnp.zeros_like(part[..., :1, :]))

    def along_x(part):
        return diff_down(part, -1, jnp.zeros_like(part[..., :1]))

    def along_z(part, face):
        return diff_down(part, -3, face[..., None, :, :])

    comp_x, comp_y, comp_z = field[:, 0], field[:, 1], field[:, 2]
    first = along_y(comp_z) - along_z(comp_y, lower_face[:, 1])
    second = along_z(comp_x, lower_face[:, 0]) - along_x(comp_z)
    third = along_x(comp_y) - along_y(comp_x)
    return jnp.stack([first, second, third], axis=1)


def jacobi_update(field_grid, rhs_grid, curl_electric, curl_magnetic, displacement, angular, eps_grid):
    elec_re, elec_im = field_grid[0, :3], field_grid[1, :3]
    mag_re, mag_im = field_grid[0, 3:], field_grid[1, 3:]
    res_elec_re = rhs_grid[0, :3] + angular * displacement[1] + curl_magnetic[0]
    res_elec_im = rhs_grid[1, :3] - angular * displacement[0] + curl_magnetic[1]
    res_mag_re = rhs_grid[0, 3:] - curl_electric[0] + angular * mag_im
    res_mag_im = rhs_grid[1, 3:] - curl_electric[1] - angular * mag_re
    scale_elec = angular * eps_grid
    new_re = jnp.concatenate([elec_re + res_elec_im / scale_elec, mag_re + res_mag_im / angular], axis=0)
    new_im = jnp.concatenate([elec_im - res_elec_re / scale_elec, mag_im - res_mag_re / angular], axis=0)
    return jnp.stack([new_re, new_im], axis=0)


def jacobi_sweep(fields, rhs_field, permittivity, strength, cosine, sine_part):
    eps_grid = permittivity.reshape(PLANES, TY, TX)
    electric_all = fields[:, :3]

    def per_harmonic(harmonic):
        current = lax.dynamic_index_in_dim(fields, harmonic, axis=2, keepdims=False)
        rhs_now = lax.dynamic_index_in_dim(rhs_field, harmonic, axis=2, keepdims=False)
        lower_band = lax.dynamic_index_in_dim(electric_all, jnp.maximum(harmonic - 1, 0), axis=2, keepdims=False)
        lower_band = lower_band * (harmonic > 0).astype(fields.dtype)
        upper_band = lax.dynamic_index_in_dim(electric_all, jnp.minimum(harmonic + 1, HARMONICS - 1), axis=2, keepdims=False)
        upper_band = upper_band * (harmonic < HARMONICS - 1).astype(fields.dtype)
        angular = BASE_FREQUENCY + MOD_FREQUENCY * (harmonic - HARMONICS // 2).astype(fields.dtype)
        half_strength = strength * 0.5
        electric = current[:, :3]
        couple_re = half_strength * (cosine * (lower_band[0] + upper_band[0]) + sine_part * (upper_band[1] - lower_band[1]))
        couple_im = half_strength * (cosine * (lower_band[1] + upper_band[1]) + sine_part * (lower_band[0] - upper_band[0]))
        displace_re = permittivity * electric[0] + couple_re
        displace_im = permittivity * electric[1] + couple_im
        displacement = jnp.stack([displace_re, displace_im]).reshape(2, 3, PLANES, TY, TX)
        field_grid = current.reshape(2, 6, PLANES, TY, TX)
        rhs_grid = rhs_now.reshape(2, 6, PLANES, TY, TX)
        zero_face = jnp.zeros((2, 2, TY, TX), fields.dtype)
        curl_electric = curl_up(field_grid[:, :3], zero_face)
        curl_magnetic = curl_down(field_grid[:, 3:], zero_face)
        updated = jacobi_update(field_grid, rhs_grid, curl_electric, curl_magnetic, displacement, angular, eps_grid)
        return updated.reshape(2, 6, CELLS)

    stacked = lax.map(per_harmonic, jnp.arange(HARMONICS, dtype=jnp.int32))
    return jnp.transpose(stacked, (1, 2, 0, 3))


def reference(rhs_field, field_guess, permittivity, mod_cells, mod_count, mod_profile, mod_amp, mod_phase):
    active = jnp.arange(MOD_CAP, dtype=jnp.int32)[None, :] < mod_count[:, None]
    strength_list = jnp.where(active, mod_amp[mod_profile], 0.0)
    slab_index = jnp.arange(SLABS, dtype=jnp.int32)[:, None]
    plane_index = slab_index * PLANES_DEV + mod_cells // (TY * TX)
    phase_angle = mod_phase[mod_profile] - WAVE_NUMBER * plane_index.astype(mod_phase.dtype)
    scatter_at = (slab_index * CELLS_DEV + mod_cells).astype(jnp.int32).reshape(-1)
    empty = jnp.zeros((CELLS,), rhs_field.dtype)
    strength = empty.at[scatter_at].add(strength_list.reshape(-1))
    cosine = empty.at[scatter_at].add(jnp.cos(phase_angle).reshape(-1))
    sine_part = empty.at[scatter_at].add(jnp.sin(phase_angle).reshape(-1))
    fields = field_guess
    for sweep_index in range(ITERS):
        fields = jacobi_sweep(fields, rhs_field, permittivity, strength, cosine, sine_part)
    return fields
```

```python
import functools

import jax
import jax.numpy as jnp
from jax import lax
from jax.experimental import pallas as pl
from jax.experimental.pallas import tpu as pltpu
from jax.sharding import PartitionSpec as P

HARMONICS = 64
TX = 64
BASE_FREQUENCY = 6.0
MOD_FREQUENCY = 0.05
WAVE_NUMBER = 0.3
PROFILES = 16
MESH = pl.DeviceIdType.MESH
LANES = 128
BLOCK = 512
CHUNKS = 8


def remote(src, dst, send, recv, device):
    return pltpu.make_async_remote_copy(
        src_ref=src, dst_ref=dst, send_sem=send, recv_sem=recv, device_id=device, device_id_type=MESH
    )


def signal(condition, sem, device):
    @pl.when(condition)
    def _():
        pl.semaphore_signal(sem, inc=1, device_id=device, device_id_type=MESH)


def mod_tables(plane, cells, profile, count, amp, phase):
    row = lax.broadcasted_iota(jnp.int32, (PROFILES, LANES), 0)
    amps = jnp.zeros((PROFILES, LANES), jnp.float32)
    phases = jnp.zeros((PROFILES, LANES), jnp.float32)
    for i in range(PROFILES):
        amps = jnp.where(row == i, amp[i], amps)
        phases = jnp.where(row == i, phase[i], phases)
    angle = phases - WAVE_NUMBER * plane
    cosines = 0.5 * amps * jnp.cos(angle)
    sines = 0.5 * amps * jnp.sin(angle)
    length = cells.shape[1]
    live = count[0]
    lane = lax.broadcasted_iota(jnp.int32, (1, LANES), 1)
    low_row = lax.broadcasted_iota(jnp.int32, (LANES, LANES), 0)
    left, right = [], []
    for j in range(length // LANES):
        part = slice(j * LANES, (j + 1) * LANES)
        cell, prof = cells[:, part], profile[:, part]
        active = (lane + j * LANES) < live
        here = (row == cell // LANES) & active
        hit = row == prof
        cosine = jnp.sum(jnp.where(hit, cosines, 0.0), axis=0, keepdims=True)
        sine = jnp.sum(jnp.where(hit, sines, 0.0), axis=0, keepdims=True)
        left.append(
            jnp.concatenate([jnp.where(here, cosine, 0.0), jnp.where(here, sine, 0.0)], axis=0)
        )
        right.append((low_row == cell % LANES).astype(jnp.float32))
    return lax.dot_general(
        jnp.concatenate(left, axis=1),
        jnp.concatenate(right, axis=1),
        (((1,), (1,)), ((), ())),
        precision=lax.Precision.HIGHEST,
        preferred_element_type=jnp.float32,
    )


def partial_sweep(fields, rhs, low_edge, high_edge, tab, a, out, cells):
    width = min(BLOCK, cells)
    wide = width + LANES
    lane = lax.broadcasted_iota(jnp.int32, (8, width), 1)
    column = lane % TX
    not_last, not_first = column != TX - 1, column != 0
    row = lax.broadcasted_iota(jnp.int32, (8, width), 0)

    def body(step, carry):
        at = pl.multiple_of(step * width, LANES)
        here = pl.ds(at, width)
        mid = pl.ds(pl.multiple_of(at + LANES, LANES), width)

        def ahead(c, k):
            v = fields[c, k, :, pl.ds(pl.multiple_of(at + LANES, LANES), wide)]
            own = v[:, :width]
            dy = pltpu.roll(v, wide - TX, 1)[:, :width] - own
            dx = jnp.where(not_last, pltpu.roll(v, wide - 1, 1)[:, :width], 0.0) - own
            return own, dy, dx

        def behind(c, k):
            v = fields[c, k, :, pl.ds(at, wide)]
            own = v[:, LANES:]
            dy = own - pltpu.roll(v, TX, 1)[:, LANES:]
            dx = own - jnp.where(not_first, pltpu.roll(v, 1, 1)[:, LANES:], 0.0)
            return own, dy, dx

        cos_t, sin_t, ae = (tab[i, :, here] for i in range(3))
        couple = []
        for k in range(3):
            low, high = [], []
            for c in range(2):
                v = fields[c, k, :, mid]
                i = c * 3 + k
                low.append(jnp.where(row == 0, low_edge[i : i + 1, here], pltpu.roll(v, 1, 0)))
                high.append(jnp.where(row == 7, high_edge[i : i + 1, here], pltpu.roll(v, 7, 0)))
            couple.append(
                (
                    cos_t * (low[0] + high[0]) + sin_t * (high[1] - low[1]),
                    cos_t * (low[1] + high[1]) + sin_t * (low[0] - high[0]),
                )
            )
        for c in range(2):
            s = 1.0 if c == 1 else -1.0
            ex, ex_y, _ = ahead(c, 0)
            ey, _, ey_x = ahead(c, 1)
            _, ez_y, ez_x = ahead(c, 2)
            sa = s * a
            out(3, 1 - c, here, sa * (rhs[c, 3, :, here] - ez_y - ey))
            out(4, 1 - c, here, sa * (rhs[c, 4, :, here] + ex + ez_x))
            out(5, 1 - c, here, sa * (rhs[c, 5, :, here] - ey_x + ex_y))
            hx, hx_y, _ = behind(c, 3)
            hy, _, hy_x = behind(c, 4)
            _, hz_y, hz_x = behind(c, 5)
            sae = s * ae
            out(0, 1 - c, here, sae * (rhs[c, 0, :, here] + hz_y - hy) - couple[0][1 - c])
            out(1, 1 - c, here, sae * (rhs[c, 1, :, here] + hx - hz_x) - couple[1][1 - c])
            out(2, 1 - c, here, sae * (rhs[c, 2, :, here] + hy_x - hx_y) - couple[2][1 - c])
        return carry

    lax.fori_loop(0, cells // width, body, 0)


def kernel(
    rhs_hbm, field_hbm, eps_hbm, cells_hbm, profile_hbm, count, amp, phase, out_hbm,
    x, y, rhs, res, p_own, q_own, e_next, h_prev, p_next, q_prev, eps, eps_next, cells, profile,
    tab, low_out, high_out, low_in, high_in,
    local_sem, out_sem, eps_sem, edge_send, edge_recv, down_send, down_recv, up_send, up_recv,
):
    h, p = lax.axis_index("harm"), lax.axis_index("prop")
    nh, np_ = lax.axis_size("harm"), lax.axis_size("prop")
    size = rhs.shape[3]
    chunk = size // CHUNKS
    below, above = {"prop": p - 1}, {"prop": p + 1}
    has_below, has_above = p > 0, p < np_ - 1
    has_low, has_high = h > 0, h < nh - 1

    barrier = pltpu.get_barrier_semaphore()
    signal(has_below, barrier, below)
    signal(has_above, barrier, above)
    signal(has_low, barrier, {"harm": h - 1})
    signal(has_high, barrier, {"harm": h + 1})

    interior = slice(LANES, LANES + size)
    loads = [
        pltpu.make_async_copy(field_hbm, x.at[:, :, :, interior], local_sem.at[0]),
        pltpu.make_async_copy(rhs_hbm, rhs, local_sem.at[1]),
        pltpu.make_async_copy(eps_hbm, eps, local_sem.at[2]),
        pltpu.make_async_copy(cells_hbm, cells, local_sem.at[3]),
        pltpu.make_async_copy(profile_hbm, profile, local_sem.at[4]),
    ]
    for load in loads:
        load.start()

    neighbours = (
        has_below.astype(jnp.int32) + has_above.astype(jnp.int32)
        + has_low.astype(jnp.int32) + has_high.astype(jnp.int32)
    )
    pl.semaphore_wait(barrier, neighbours)

    def lanes(c):
        return slice(c * chunk, (c + 1) * chunk)

    def down(sweep, c):
        src = field_hbm.at[:, 0:2, :, lanes(c)] if sweep == 0 else p_own.at[:, :, :, lanes(c)]
        dst = (e_next, p_next)[sweep].at[:, :, :, lanes(c)]
        return remote(src, dst, down_send.at[sweep, c], down_recv.at[sweep, c], below)

    def up(sweep, c):
        src = field_hbm.at[:, 3:5, :, lanes(c)] if sweep == 0 else q_own.at[:, :, :, lanes(c)]
        dst = (h_prev, q_prev)[sweep].at[:, :, :, lanes(c)]
        return remote(src, dst, up_send.at[sweep, c], up_recv.at[sweep, c], above)

    eps_copy = remote(eps_hbm, eps_next, eps_sem.at[0], eps_sem.at[1], below)

    def start_sweep(sweep):
        for c in range(CHUNKS):

            @pl.when(has_below)
            def _():
                down(sweep, c).start()

            @pl.when(has_above)
            def _():
                up(sweep, c).start()

    start_sweep(0)

    @pl.when(has_below)
    def _():
        eps_copy.start()

    def to_low(sweep):
        return remote(
            low_out.at[sweep], high_in.at[sweep], edge_send.at[sweep, 0], edge_recv.at[sweep, 0],
            {"harm": h - 1},
        )

    def to_high(sweep):
        return remote(
            high_out.at[sweep], low_in.at[sweep], edge_send.at[sweep, 1], edge_recv.at[sweep, 1],
            {"harm": h + 1},
        )

    def send_edges(sweep, fields):
        for c in range(2):
            for k in range(3):
                i = c * 3 + k
                low_out[sweep, i : i + 1, :] = fields[c, k, 0:1, interior]
                high_out[sweep, i : i + 1, :] = fields[c, k, 7:8, interior]

        @pl.when(has_low)
        def _():
            to_low(sweep).start()

        @pl.when(has_high)
        def _():
            to_high(sweep).start()

    def wait_edges(sweep):
        @pl.when(has_high)
        def _():
            to_low(sweep).wait_recv()

        @pl.when(has_low)
        def _():
            to_high(sweep).wait_recv()

    for sweep in range(2):
        low_out[sweep, 6:8, :] = jnp.zeros((2, size), jnp.float32)
        high_out[sweep, 6:8, :] = jnp.zeros((2, size), jnp.float32)
    loads[0].wait()
    send_edges(0, x)

    @pl.when(jnp.logical_not(has_low))
    def _():
        low_in[...] = jnp.zeros_like(low_in)

    @pl.when(jnp.logical_not(has_high))
    def _():
        high_in[...] = jnp.zeros_like(high_in)

    @pl.when(jnp.logical_not(has_below))
    def _():
        h_prev[...] = jnp.zeros_like(h_prev)
        q_prev[...] = jnp.zeros_like(q_prev)

    @pl.when(jnp.logical_not(has_above))
    def _():
        e_next[...] = jnp.zeros_like(e_next)
        p_next[...] = jnp.zeros_like(p_next)
        eps_next[...] = jnp.ones_like(eps_next)

    pad = jnp.zeros((2, 3, 8, LANES), jnp.float32)
    for fields in (x, y):
        fields[:, 0:3, :, LANES + size :] = pad
        fields[:, 3:6, :, :LANES] = pad

    harmonic = h * 8 + lax.broadcasted_iota(jnp.int32, (8, 1), 0)
    omega = BASE_FREQUENCY + MOD_FREQUENCY * (harmonic - HARMONICS // 2).astype(jnp.float32)
    a = 1.0 / omega
    for load in loads[2:]:
        load.wait()
    dense = mod_tables(p.astype(jnp.float32), cells[...], profile[...], count, amp, phase)
    for i in range(size // LANES):
        part = slice(i * LANES, (i + 1) * LANES)
        inverse = 1.0 / eps[:, part]
        tab[0, :, part] = jnp.broadcast_to(dense[i : i + 1, :] * inverse, (8, LANES))
        tab[1, :, part] = jnp.broadcast_to(dense[PROFILES + i : PROFILES + i + 1, :] * inverse, (8, LANES))
        tab[2, :, part] = a * inverse
    loads[1].wait()
    wait_edges(0)

    def to_first(k, c, here, value):
        if k in (0, 1):
            p_own[c, k, :, here] = value
        elif k in (3, 4):
            q_own[c, k - 3, :, here] = value
        else:
            y[c, k, :, pl.ds(pl.multiple_of(here.start + LANES, LANES), here.size)] = value

    partial_sweep(x, rhs, low_in.at[0], high_in.at[0], tab, a, to_first, size)
    start_sweep(1)

    for c in range(CHUNKS):

        @pl.when(has_above)
        def _():
            down(0, c).wait_recv()

        @pl.when(has_below)
        def _():
            up(0, c).wait_recv()

        part = lanes(c)
        wide = slice(LANES + c * chunk, LANES + (c + 1) * chunk)
        ae = tab[2, :, part]
        for i in range(2):
            s = 1.0 if i == 1 else -1.0
            y[1 - i, 0, :, wide] = p_own[1 - i, 0, :, part] + s * ae * h_prev[i, 1, :, part]
            y[1 - i, 1, :, wide] = p_own[1 - i, 1, :, part] - s * ae * h_prev[i, 0, :, part]
            y[1 - i, 3, :, wide] = q_own[1 - i, 0, :, part] + s * a * e_next[i, 1, :, part]
            y[1 - i, 4, :, wide] = q_own[1 - i, 1, :, part] - s * a * e_next[i, 0, :, part]

    send_edges(1, y)

    @pl.when(has_above)
    def _():
        eps_copy.wait_recv()

    above_factor = has_above.astype(jnp.float32)
    below_factor = has_below.astype(jnp.float32)
    wait_edges(1)

    def to_second(k, c, here, value):
        res[c, k, :, here] = value

    partial_sweep(y, rhs, low_in.at[1], high_in.at[1], tab, a, to_second, size)
    outs = [
        pltpu.make_async_copy(res.at[:, k], out_hbm.at[:, k], out_sem.at[0, i])
        for i, k in enumerate((2, 5))
    ]
    for copy in outs:
        copy.start()

    for c in range(CHUNKS):
        part = lanes(c)
        wide = slice(LANES + c * chunk, LANES + (c + 1) * chunk)

        @pl.when(has_above)
        def _():
            down(1, c).wait_recv()

        @pl.when(has_below)
        def _():
            up(1, c).wait_recv()

        ae = tab[2, :, part]
        ae_next = a * (above_factor / eps_next[:, part])
        a_below = a * below_factor
        for i in range(2):
            s = 1.0 if i == 1 else -1.0
            j = 1 - i
            ex = p_next[i, 0, :, part] - s * ae_next * x[j, 4, :, wide]
            ey = p_next[i, 1, :, part] + s * ae_next * x[j, 3, :, wide]
            hx = q_prev[i, 0, :, part] - s * a_below * x[j, 1, :, wide]
            hy = q_prev[i, 1, :, part] + s * a_below * x[j, 0, :, wide]
            res[j, 0, :, part] += s * ae * hy
            res[j, 1, :, part] -= s * ae * hx
            res[j, 3, :, part] += s * a * ey
            res[j, 4, :, part] -= s * a * ex
        for i, k in enumerate((0, 3)):
            copy = pltpu.make_async_copy(
                res.at[:, k : k + 2, :, part], out_hbm.at[:, k : k + 2, :, part], out_sem.at[c + 1, i]
            )
            copy.start()
            outs.append(copy)

    @pl.when(has_below)
    def _():
        eps_copy.wait_send()

    for sweep in range(2):

        @pl.when(has_low)
        def _():
            to_low(sweep).wait_send()

        @pl.when(has_high)
        def _():
            to_high(sweep).wait_send()

        for c in range(CHUNKS):

            @pl.when(has_below)
            def _():
                down(sweep, c).wait_send()

            @pl.when(has_above)
            def _():
                up(sweep, c).wait_send()

    for copy in outs:
        copy.wait()


def local(rhs_field, field_guess, permittivity, mod_cells, mod_count, mod_profile, mod_amp, mod_phase):
    size = permittivity.shape[0]
    listed = mod_cells.shape[1]
    f32 = jnp.float32
    whole = (2, 6, 8, size)
    padded = (2, 6, 8, size + 2 * LANES)
    face = (2, 2, 8, size)
    dma = pltpu.SemaphoreType.DMA
    anywhere, smem = pl.BlockSpec(memory_space=pl.ANY), pl.BlockSpec(memory_space=pltpu.SMEM)
    return pl.pallas_call(
        kernel,
        out_shape=jax.ShapeDtypeStruct(whole, f32),
        in_specs=[anywhere] * 5 + [smem] * 3,
        out_specs=anywhere,
        scratch_shapes=[
            pltpu.VMEM(padded, f32), pltpu.VMEM(padded, f32), pltpu.VMEM(whole, f32), pltpu.VMEM(whole, f32),
            *[pltpu.VMEM(face, f32)] * 6,
            pltpu.VMEM((1, size), f32), pltpu.VMEM((1, size), f32),
            pltpu.VMEM((1, listed), jnp.int32), pltpu.VMEM((1, listed), jnp.int32),
            pltpu.VMEM((3, 8, size), f32),
            *[pltpu.VMEM((2, 8, size), f32)] * 4,
            dma((5,)), dma((CHUNKS + 1, 2)), dma((2,)), dma((2, 2)), dma((2, 2)),
            *[dma((2, CHUNKS))] * 4,
        ],
        compiler_params=pltpu.CompilerParams(
            collective_id=0, has_side_effects=True, vmem_limit_bytes=60 * 2**20
        ),
        name="sweeps",
    )(rhs_field, field_guess, permittivity.reshape(1, size), mod_cells, mod_profile, mod_count, mod_amp, mod_phase)


def solution(mesh):
    return jax.shard_map(
        local,
        mesh=mesh,
        in_specs=(
            P(None, None, "harm", "prop"),
            P(None, None, "harm", "prop"),
            P("prop"),
            P("prop", None),
            P("prop"),
            P("prop", None),
            P(),
            P(),
        ),
        out_specs=P(None, None, "harm", "prop"),
        check_vma=False,
    )
```

```python
import functools

import jax
import jax.numpy as jnp
from jax import lax
from jax.experimental import pallas as pl
from jax.experimental.pallas import tpu as pltpu
from jax.sharding import PartitionSpec as P

HARMONICS = 64
TX = 64
BASE_FREQUENCY = 6.0
MOD_FREQUENCY = 0.05
WAVE_NUMBER = 0.3
PROFILES = 16
MESH = pl.DeviceIdType.MESH
LANES = 128
BLOCK = 512
CHUNKS = 8
LAST = 15
UP_BY, DOWN_BY = (0, 3), (31, 28)
WAYS = ((1, 2, 0, 1, 2, 0, 1, 0), (1, 2, 0, 2, 1, 0, 2, 0))
SLOTS = 3
RELAYED = [
    (sweep, c, way, WAYS[sweep][:c].count(way))
    for sweep in range(2)
    for c, way in enumerate(WAYS[sweep])
    if way
]


def remote(src, dst, send, recv, device):
    return pltpu.make_async_remote_copy(
        src_ref=src, dst_ref=dst, send_sem=send, recv_sem=recv, device_id=device, device_id_type=MESH
    )


def signal(condition, sem, device):
    @pl.when(condition)
    def _():
        pl.semaphore_signal(sem, inc=1, device_id=device, device_id_type=MESH)


def mod_tables(plane, cells, profile, count, amp, phase):
    row = lax.broadcasted_iota(jnp.int32, (PROFILES, LANES), 0)
    amps = jnp.zeros((PROFILES, LANES), jnp.float32)
    phases = jnp.zeros((PROFILES, LANES), jnp.float32)
    for i in range(PROFILES):
        amps = jnp.where(row == i, amp[i], amps)
        phases = jnp.where(row == i, phase[i], phases)
    angle = phases - WAVE_NUMBER * plane
    cosines = 0.5 * amps * jnp.cos(angle)
    sines = 0.5 * amps * jnp.sin(angle)
    length = cells.shape[1]
    live = count[0]
    lane = lax.broadcasted_iota(jnp.int32, (1, LANES), 1)
    low_row = lax.broadcasted_iota(jnp.int32, (LANES, LANES), 0)
    left, right = [], []
    for j in range(length // LANES):
        part = slice(j * LANES, (j + 1) * LANES)
        cell, prof = cells[:, part], profile[:, part]
        active = (lane + j * LANES) < live
        here = (row == cell // LANES) & active
        hit = row == prof
        cosine = jnp.sum(jnp.where(hit, cosines, 0.0), axis=0, keepdims=True)
        sine = jnp.sum(jnp.where(hit, sines, 0.0), axis=0, keepdims=True)
        left.append(
            jnp.concatenate([jnp.where(here, cosine, 0.0), jnp.where(here, sine, 0.0)], axis=0)
        )
        right.append((low_row == cell % LANES).astype(jnp.float32))
    return lax.dot_general(
        jnp.concatenate(left, axis=1),
        jnp.concatenate(right, axis=1),
        (((1,), (1,)), ((), ())),
        precision=lax.Precision.HIGHEST,
        preferred_element_type=jnp.float32,
    )


def partial_sweep(fields, rhs, low_edge, high_edge, tab, a, out, cells):
    width = min(BLOCK, cells)
    wide = width + LANES
    lane = lax.broadcasted_iota(jnp.int32, (8, width), 1)
    column = lane % TX
    not_last, not_first = column != TX - 1, column != 0
    row = lax.broadcasted_iota(jnp.int32, (8, width), 0)

    def body(step, carry):
        at = pl.multiple_of(step * width, LANES)
        here = pl.ds(at, width)
        mid = pl.ds(pl.multiple_of(at + LANES, LANES), width)

        def ahead(c, k):
            v = fields[c, k, :, pl.ds(pl.multiple_of(at + LANES, LANES), wide)]
            own = v[:, :width]
            dy = pltpu.roll(v, wide - TX, 1)[:, :width] - own
            dx = jnp.where(not_last, pltpu.roll(v, wide - 1, 1)[:, :width], 0.0) - own
            return own, dy, dx

        def behind(c, k):
            v = fields[c, k, :, pl.ds(at, wide)]
            own = v[:, LANES:]
            dy = own - pltpu.roll(v, TX, 1)[:, LANES:]
            dx = own - jnp.where(not_first, pltpu.roll(v, 1, 1)[:, LANES:], 0.0)
            return own, dy, dx

        cos_t, sin_t, ae = (tab[i, :, here] for i in range(3))
        couple = []
        for k in range(3):
            low, high = [], []
            for c in range(2):
                v = fields[c, k, :, mid]
                i = c * 3 + k
                low.append(jnp.where(row == 0, low_edge[i : i + 1, here], pltpu.roll(v, 1, 0)))
                high.append(jnp.where(row == 7, high_edge[i : i + 1, here], pltpu.roll(v, 7, 0)))
            couple.append(
                (
                    cos_t * (low[0] + high[0]) + sin_t * (high[1] - low[1]),
                    cos_t * (low[1] + high[1]) + sin_t * (low[0] - high[0]),
                )
            )
        for c in range(2):
            s = 1.0 if c == 1 else -1.0
            ex, ex_y, _ = ahead(c, 0)
            ey, _, ey_x = ahead(c, 1)
            _, ez_y, ez_x = ahead(c, 2)
            sa = s * a
            out(3, 1 - c, here, sa * (rhs[c, 3, :, here] - ez_y - ey))
            out(4, 1 - c, here, sa * (rhs[c, 4, :, here] + ex + ez_x))
            out(5, 1 - c, here, sa * (rhs[c, 5, :, here] - ey_x + ex_y))
            hx, hx_y, _ = behind(c, 3)
            hy, _, hy_x = behind(c, 4)
            _, hz_y, hz_x = behind(c, 5)
            sae = s * ae
            out(0, 1 - c, here, sae * (rhs[c, 0, :, here] + hz_y - hy) - couple[0][1 - c])
            out(1, 1 - c, here, sae * (rhs[c, 1, :, here] + hx - hz_x) - couple[1][1 - c])
            out(2, 1 - c, here, sae * (rhs[c, 2, :, here] + hy_x - hx_y) - couple[2][1 - c])
        return carry

    lax.fori_loop(0, cells // width, body, 0)


def kernel(
    rhs_hbm, field_hbm, eps_hbm, cells_hbm, profile_hbm, count, amp, phase, out_hbm,
    x, y, rhs, res, p_own, q_own, e_next, h_prev, p_next, q_prev, eps, eps_next, cells, profile,
    tab, low_out, high_out, low_in, high_in,
    passing, pass_recv, pass_send, local_sem, out_sem, eps_sem, edge_send, edge_recv, down_send, down_recv, up_send, up_recv,
):
    h, p = lax.axis_index("harm"), lax.axis_index("prop")
    nh, np_ = lax.axis_size("harm"), lax.axis_size("prop")
    size = rhs.shape[3]
    chunk = size // CHUNKS
    below, above = {"prop": p - 1}, {"prop": p + 1}
    has_below, has_above = p > 0, p < np_ - 1
    has_low, has_high = h > 0, h < nh - 1

    barrier = pltpu.get_barrier_semaphore()
    signal(has_below, barrier, below)
    signal(has_above, barrier, above)
    signal(has_low, barrier, {"harm": h - 1})
    signal(has_high, barrier, {"harm": h + 1})

    interior = slice(LANES, LANES + size)
    loads = [
        pltpu.make_async_copy(field_hbm, x.at[:, :, :, interior], local_sem.at[0]),
        pltpu.make_async_copy(rhs_hbm, rhs, local_sem.at[1]),
        pltpu.make_async_copy(eps_hbm, eps, local_sem.at[2]),
        pltpu.make_async_copy(cells_hbm, cells, local_sem.at[3]),
        pltpu.make_async_copy(profile_hbm, profile, local_sem.at[4]),
    ]
    for load in loads:
        load.start()

    neighbours = (
        has_below.astype(jnp.int32) + has_above.astype(jnp.int32)
        + has_low.astype(jnp.int32) + has_high.astype(jnp.int32)
    )
    far = [(LAST, by, LAST + 1) for by in UP_BY] + [(LAST + 1, by, LAST) for by in DOWN_BY]
    for start, by, end in far:
        signal(p == by, barrier, {"prop": start})
        signal(p == end, barrier, {"prop": by})
        neighbours += (p == start).astype(jnp.int32) + (p == by).astype(jnp.int32)
    pl.semaphore_wait(barrier, neighbours)

    def lanes(c):
        return slice(c * chunk, (c + 1) * chunk)

    def down_parts(sweep, c):
        src = field_hbm.at[:, 0:2, :, lanes(c)] if sweep == 0 else p_own.at[:, :, :, lanes(c)]
        dst = (e_next, p_next)[sweep].at[:, :, :, lanes(c)]
        return src, dst, down_send.at[sweep, c], down_recv.at[sweep, c]

    def down(sweep, c):
        return remote(*down_parts(sweep, c), below)

    def up_parts(sweep, c):
        src = field_hbm.at[:, 3:5, :, lanes(c)] if sweep == 0 else q_own.at[:, :, :, lanes(c)]
        dst = (h_prev, q_prev)[sweep].at[:, :, :, lanes(c)]
        return src, dst, up_send.at[sweep, c], up_recv.at[sweep, c]

    def up(sweep, c):
        return remote(*up_parts(sweep, c), above)

    eps_copy = remote(eps_hbm, eps_next, eps_sem.at[0], eps_sem.at[1], below)

    def to_pass(sweep, c, i, is_up, by):
        src, _, send, _ = (up_parts if is_up else down_parts)(sweep, c)
        return remote(src, passing.at[sweep, i], send, pass_recv.at[sweep, i], {"prop": by})

    def pass_on(sweep, c, i, is_up):
        _, dst, _, recv = (up_parts if is_up else down_parts)(sweep, c)
        end = LAST + 1 if is_up else LAST
        return remote(passing.at[sweep, i], dst, pass_send.at[sweep, i], recv, {"prop": end})

    def start_sweep(sweep):
        for at, c, way, i in RELAYED:
            if at == sweep:
                for is_up, start, by in ((True, LAST, UP_BY[way - 1]), (False, LAST + 1, DOWN_BY[way - 1])):

                    @pl.when(p == start)
                    def _():
                        to_pass(sweep, c, i, is_up, by).start()

        for c in range(CHUNKS):
            straight = WAYS[sweep][c] == 0

            @pl.when(has_below if straight else has_below & (p != LAST + 1))
            def _():
                down(sweep, c).start()

            @pl.when(has_above if straight else has_above & (p != LAST))
            def _():
                up(sweep, c).start()

    def pass_all(sweep):
        for at, c, way, i in RELAYED:
            if at == sweep:
                for is_up, by in ((True, UP_BY[way - 1]), (False, DOWN_BY[way - 1])):

                    @pl.when(p == by)
                    def _():
                        to_pass(sweep, c, i, is_up, by).wait_recv()
                        pass_on(sweep, c, i, is_up).start()

    start_sweep(0)

    @pl.when(has_below)
    def _():
        eps_copy.start()

    def to_low(sweep):
        return remote(
            low_out.at[sweep], high_in.at[sweep], edge_send.at[sweep, 0], edge_recv.at[sweep, 0],
            {"harm": h - 1},
        )

    def to_high(sweep):
        return remote(
            high_out.at[sweep], low_in.at[sweep], edge_send.at[sweep, 1], edge_recv.at[sweep, 1],
            {"harm": h + 1},
        )

    def send_edges(sweep, fields):
        for c in range(2):
            for k in range(3):
                i = c * 3 + k
                low_out[sweep, i : i + 1, :] = fields[c, k, 0:1, interior]
                high_out[sweep, i : i + 1, :] = fields[c, k, 7:8, interior]

        @pl.when(has_low)
        def _():
            to_low(sweep).start()

        @pl.when(has_high)
        def _():
            to_high(sweep).start()

    def wait_edges(sweep):
        @pl.when(has_high)
        def _():
            to_low(sweep).wait_recv()

        @pl.when(has_low)
        def _():
            to_high(sweep).wait_recv()

    for sweep in range(2):
        low_out[sweep, 6:8, :] = jnp.zeros((2, size), jnp.float32)
        high_out[sweep, 6:8, :] = jnp.zeros((2, size), jnp.float32)
    loads[0].wait()
    send_edges(0, x)

    @pl.when(jnp.logical_not(has_low))
    def _():
        low_in[...] = jnp.zeros_like(low_in)

    @pl.when(jnp.logical_not(has_high))
    def _():
        high_in[...] = jnp.zeros_like(high_in)

    @pl.when(jnp.logical_not(has_below))
    def _():
        h_prev[...] = jnp.zeros_like(h_prev)
        q_prev[...] = jnp.zeros_like(q_prev)

    @pl.when(jnp.logical_not(has_above))
    def _():
        e_next[...] = jnp.zeros_like(e_next)
        p_next[...] = jnp.zeros_like(p_next)
        eps_next[...] = jnp.ones_like(eps_next)

    pad = jnp.zeros((2, 3, 8, LANES), jnp.float32)
    for fields in (x, y):
        fields[:, 0:3, :, LANES + size :] = pad
        fields[:, 3:6, :, :LANES] = pad

    harmonic = h * 8 + lax.broadcasted_iota(jnp.int32, (8, 1), 0)
    omega = BASE_FREQUENCY + MOD_FREQUENCY * (harmonic - HARMONICS // 2).astype(jnp.float32)
    a = 1.0 / omega
    for load in loads[2:]:
        load.wait()
    dense = mod_tables(p.astype(jnp.float32), cells[...], profile[...], count, amp, phase)
    for i in range(size // LANES):
        part = slice(i * LANES, (i + 1) * LANES)
        inverse = 1.0 / eps[:, part]
        tab[0, :, part] = jnp.broadcast_to(dense[i : i + 1, :] * inverse, (8, LANES))
        tab[1, :, part] = jnp.broadcast_to(dense[PROFILES + i : PROFILES + i + 1, :] * inverse, (8, LANES))
        tab[2, :, part] = a * inverse
    loads[1].wait()
    wait_edges(0)

    def to_first(k, c, here, value):
        if k in (0, 1):
            p_own[c, k, :, here] = value
        elif k in (3, 4):
            q_own[c, k - 3, :, here] = value
        else:
            y[c, k, :, pl.ds(pl.multiple_of(here.start + LANES, LANES), here.size)] = value

    partial_sweep(x, rhs, low_in.at[0], high_in.at[0], tab, a, to_first, size)
    start_sweep(1)

    for c in range(CHUNKS):

        @pl.when(has_above)
        def _():
            down(0, c).wait_recv()

        @pl.when(has_below)
        def _():
            up(0, c).wait_recv()

        part = lanes(c)
        wide = slice(LANES + c * chunk, LANES + (c + 1) * chunk)
        ae = tab[2, :, part]
        for i in range(2):
            s = 1.0 if i == 1 else -1.0
            y[1 - i, 0, :, wide] = p_own[1 - i, 0, :, part] + s * ae * h_prev[i, 1, :, part]
            y[1 - i, 1, :, wide] = p_own[1 - i, 1, :, part] - s * ae * h_prev[i, 0, :, part]
            y[1 - i, 3, :, wide] = q_own[1 - i, 0, :, part] + s * a * e_next[i, 1, :, part]
            y[1 - i, 4, :, wide] = q_own[1 - i, 1, :, part] - s * a * e_next[i, 0, :, part]

    send_edges(1, y)
    pass_all(0)
    pass_all(1)

    @pl.when(has_above)
    def _():
        eps_copy.wait_recv()

    above_factor = has_above.astype(jnp.float32)
    below_factor = has_below.astype(jnp.float32)
    wait_edges(1)

    def to_second(k, c, here, value):
        res[c, k, :, here] = value

    partial_sweep(y, rhs, low_in.at[1], high_in.at[1], tab, a, to_second, size)
    outs = [
        pltpu.make_async_copy(res.at[:, k], out_hbm.at[:, k], out_sem.at[0, i])
        for i, k in enumerate((2, 5))
    ]
    for copy in outs:
        copy.start()

    for c in range(CHUNKS):
        part = lanes(c)
        wide = slice(LANES + c * chunk, LANES + (c + 1) * chunk)

        @pl.when(has_above)
        def _():
            down(1, c).wait_recv()

        @pl.when(has_below)
        def _():
            up(1, c).wait_recv()

        ae = tab[2, :, part]
        ae_next = a * (above_factor / eps_next[:, part])
        a_below = a * below_factor
        for i in range(2):
            s = 1.0 if i == 1 else -1.0
            j = 1 - i
            ex = p_next[i, 0, :, part] - s * ae_next * x[j, 4, :, wide]
            ey = p_next[i, 1, :, part] + s * ae_next * x[j, 3, :, wide]
            hx = q_prev[i, 0, :, part] - s * a_below * x[j, 1, :, wide]
            hy = q_prev[i, 1, :, part] + s * a_below * x[j, 0, :, wide]
            res[j, 0, :, part] += s * ae * hy
            res[j, 1, :, part] -= s * ae * hx
            res[j, 3, :, part] += s * a * ey
            res[j, 4, :, part] -= s * a * ex
        for i, k in enumerate((0, 3)):
            copy = pltpu.make_async_copy(
                res.at[:, k : k + 2, :, part], out_hbm.at[:, k : k + 2, :, part], out_sem.at[c + 1, i]
            )
            copy.start()
            outs.append(copy)

    @pl.when(has_below)
    def _():
        eps_copy.wait_send()

    for sweep in range(2):

        @pl.when(has_low)
        def _():
            to_low(sweep).wait_send()

        @pl.when(has_high)
        def _():
            to_high(sweep).wait_send()

        for c in range(CHUNKS):

            @pl.when(has_below)
            def _():
                down(sweep, c).wait_send()

            @pl.when(has_above)
            def _():
                up(sweep, c).wait_send()

    for sweep, c, way, i in RELAYED:
        for is_up, by in ((True, UP_BY[way - 1]), (False, DOWN_BY[way - 1])):

            @pl.when(p == by)
            def _():
                pass_on(sweep, c, i, is_up).wait_send()

    for copy in outs:
        copy.wait()


def local(rhs_field, field_guess, permittivity, mod_cells, mod_count, mod_profile, mod_amp, mod_phase):
    size = permittivity.shape[0]
    listed = mod_cells.shape[1]
    f32 = jnp.float32
    whole = (2, 6, 8, size)
    padded = (2, 6, 8, size + 2 * LANES)
    face = (2, 2, 8, size)
    dma = pltpu.SemaphoreType.DMA
    anywhere, smem = pl.BlockSpec(memory_space=pl.ANY), pl.BlockSpec(memory_space=pltpu.SMEM)
    return pl.pallas_call(
        kernel,
        out_shape=jax.ShapeDtypeStruct(whole, f32),
        in_specs=[anywhere] * 5 + [smem] * 3,
        out_specs=anywhere,
        scratch_shapes=[
            pltpu.VMEM(padded, f32), pltpu.VMEM(padded, f32), pltpu.VMEM(whole, f32), pltpu.VMEM(whole, f32),
            *[pltpu.VMEM(face, f32)] * 6,
            pltpu.VMEM((1, size), f32), pltpu.VMEM((1, size), f32),
            pltpu.VMEM((1, listed), jnp.int32), pltpu.VMEM((1, listed), jnp.int32),
            pltpu.VMEM((3, 8, size), f32),
            *[pltpu.VMEM((2, 8, size), f32)] * 4,
            pltpu.VMEM((2, SLOTS, 2, 2, 8, size // CHUNKS), f32), dma((2, SLOTS)), dma((2, SLOTS)),
            dma((5,)), dma((CHUNKS + 1, 2)), dma((2,)), dma((2, 2)), dma((2, 2)),
            *[dma((2, CHUNKS))] * 4,
        ],
        compiler_params=pltpu.CompilerParams(
            collective_id=0, has_side_effects=True, vmem_limit_bytes=60 * 2**20
        ),
        name="sweeps",
    )(rhs_field, field_guess, permittivity.reshape(1, size), mod_cells, mod_profile, mod_count, mod_amp, mod_phase)


def solution(mesh):
    return jax.shard_map(
        local,
        mesh=mesh,
        in_specs=(
            P(None, None, "harm", "prop"),
            P(None, None, "harm", "prop"),
            P("prop"),
            P("prop", None),
            P("prop"),
            P("prop", None),
            P(),
            P(),
        ),
        out_specs=P(None, None, "harm", "prop"),
        check_vma=False,
    )
```

```python
import functools

import jax
import jax.numpy as jnp
from jax import lax
from jax.experimental import pallas as pl
from jax.experimental.pallas import tpu as pltpu
from jax.sharding import PartitionSpec as P

HARMONICS = 64
TX = 64
BASE_FREQUENCY = 6.0
MOD_FREQUENCY = 0.05
WAVE_NUMBER = 0.3
PROFILES = 16
MESH = pl.DeviceIdType.MESH
LANES = 128
BLOCK = 512
CHUNKS = 8
LAST = 15
UP_BY, DOWN_BY = (0, 3, 12), (31, 28, 19)
WAYS = ((1, 2, 3, 0, 1, 2, 3, 0), (1, 2, 3, 0, 1, 2, 0, 0))
SLOTS = 2
RELAYED = [
    (sweep, c, way, WAYS[sweep][:c].count(way))
    for sweep in range(2)
    for c, way in enumerate(WAYS[sweep])
    if way
]


def remote(src, dst, send, recv, device):
    return pltpu.make_async_remote_copy(
        src_ref=src, dst_ref=dst, send_sem=send, recv_sem=recv, device_id=device, device_id_type=MESH
    )


def signal(condition, sem, device):
    @pl.when(condition)
    def _():
        pl.semaphore_signal(sem, inc=1, device_id=device, device_id_type=MESH)


def mod_tables(plane, cells, profile, count, amp, phase):
    row = lax.broadcasted_iota(jnp.int32, (PROFILES, LANES), 0)
    amps = jnp.zeros((PROFILES, LANES), jnp.float32)
    phases = jnp.zeros((PROFILES, LANES), jnp.float32)
    for i in range(PROFILES):
        amps = jnp.where(row == i, amp[i], amps)
        phases = jnp.where(row == i, phase[i], phases)
    angle = phases - WAVE_NUMBER * plane
    cosines = 0.5 * amps * jnp.cos(angle)
    sines = 0.5 * amps * jnp.sin(angle)
    length = cells.shape[1]
    live = count[0]
    lane = lax.broadcasted_iota(jnp.int32, (1, LANES), 1)
    low_row = lax.broadcasted_iota(jnp.int32, (LANES, LANES), 0)
    left, right = [], []
    for j in range(length // LANES):
        part = slice(j * LANES, (j + 1) * LANES)
        cell, prof = cells[:, part], profile[:, part]
        active = (lane + j * LANES) < live
        here = (row == cell // LANES) & active
        hit = row == prof
        cosine = jnp.sum(jnp.where(hit, cosines, 0.0), axis=0, keepdims=True)
        sine = jnp.sum(jnp.where(hit, sines, 0.0), axis=0, keepdims=True)
        left.append(
            jnp.concatenate([jnp.where(here, cosine, 0.0), jnp.where(here, sine, 0.0)], axis=0)
        )
        right.append((low_row == cell % LANES).astype(jnp.float32))
    return lax.dot_general(
        jnp.concatenate(left, axis=1),
        jnp.concatenate(right, axis=1),
        (((1,), (1,)), ((), ())),
        precision=lax.Precision.HIGHEST,
        preferred_element_type=jnp.float32,
    )


def partial_sweep(fields, rhs, low_edge, high_edge, tab, a, out, cells):
    width = min(BLOCK, cells)
    wide = width + LANES
    lane = lax.broadcasted_iota(jnp.int32, (8, width), 1)
    column = lane % TX
    not_last, not_first = column != TX - 1, column != 0
    row = lax.broadcasted_iota(jnp.int32, (8, width), 0)

    def body(step, carry):
        at = pl.multiple_of(step * width, LANES)
        here = pl.ds(at, width)
        mid = pl.ds(pl.multiple_of(at + LANES, LANES), width)

        def ahead(c, k):
            v = fields[c, k, :, pl.ds(pl.multiple_of(at + LANES, LANES), wide)]
            own = v[:, :width]
            dy = pltpu.roll(v, wide - TX, 1)[:, :width] - own
            dx = jnp.where(not_last, pltpu.roll(v, wide - 1, 1)[:, :width], 0.0) - own
            return own, dy, dx

        def behind(c, k):
            v = fields[c, k, :, pl.ds(at, wide)]
            own = v[:, LANES:]
            dy = own - pltpu.roll(v, TX, 1)[:, LANES:]
            dx = own - jnp.where(not_first, pltpu.roll(v, 1, 1)[:, LANES:], 0.0)
            return own, dy, dx

        cos_t, sin_t, ae = (tab[i, :, here] for i in range(3))
        couple = []
        for k in range(3):
            low, high = [], []
            for c in range(2):
                v = fields[c, k, :, mid]
                i = c * 3 + k
                low.append(jnp.where(row == 0, low_edge[i : i + 1, here], pltpu.roll(v, 1, 0)))
                high.append(jnp.where(row == 7, high_edge[i : i + 1, here], pltpu.roll(v, 7, 0)))
            couple.append(
                (
                    cos_t * (low[0] + high[0]) + sin_t * (high[1] - low[1]),
                    cos_t * (low[1] + high[1]) + sin_t * (low[0] - high[0]),
                )
            )
        for c in range(2):
            s = 1.0 if c == 1 else -1.0
            ex, ex_y, _ = ahead(c, 0)
            ey, _, ey_x = ahead(c, 1)
            _, ez_y, ez_x = ahead(c, 2)
            sa = s * a
            out(3, 1 - c, here, sa * (rhs[c, 3, :, here] - ez_y - ey))
            out(4, 1 - c, here, sa * (rhs[c, 4, :, here] + ex + ez_x))
            out(5, 1 - c, here, sa * (rhs[c, 5, :, here] - ey_x + ex_y))
            hx, hx_y, _ = behind(c, 3)
            hy, _, hy_x = behind(c, 4)
            _, hz_y, hz_x = behind(c, 5)
            sae = s * ae
            out(0, 1 - c, here, sae * (rhs[c, 0, :, here] + hz_y - hy) - couple[0][1 - c])
            out(1, 1 - c, here, sae * (rhs[c, 1, :, here] + hx - hz_x) - couple[1][1 - c])
            out(2, 1 - c, here, sae * (rhs[c, 2, :, here] + hy_x - hx_y) - couple[2][1 - c])
        return carry

    lax.fori_loop(0, cells // width, body, 0)


def kernel(
    rhs_hbm, field_hbm, eps_hbm, cells_hbm, profile_hbm, count, amp, phase, out_hbm,
    x, y, rhs, res, p_own, q_own, e_next, h_prev, p_next, q_prev, eps, eps_next, cells, profile,
    tab, low_out, high_out, low_in, high_in,
    far_sem, passing, pass_recv, pass_send, local_sem, out_sem, eps_sem, edge_send, edge_recv, down_send, down_recv, up_send, up_recv,
):
    h, p = lax.axis_index("harm"), lax.axis_index("prop")
    nh, np_ = lax.axis_size("harm"), lax.axis_size("prop")
    size = rhs.shape[3]
    chunk = size // CHUNKS
    below, above = {"prop": p - 1}, {"prop": p + 1}
    has_below, has_above = p > 0, p < np_ - 1
    has_low, has_high = h > 0, h < nh - 1

    near_above, near_below = has_above & (p != LAST), has_below & (p != LAST + 1)
    sides = [(LAST, LAST + 1, UP_BY), (LAST + 1, LAST, DOWN_BY)]
    barrier = pltpu.get_barrier_semaphore()
    signal(near_below, barrier, below)
    signal(near_above, barrier, above)
    signal(has_low, barrier, {"harm": h - 1})
    signal(has_high, barrier, {"harm": h + 1})
    neighbours = sum(
        condition.astype(jnp.int32) for condition in (near_below, near_above, has_low, has_high)
    )
    for start, end, (first, *others) in sides:
        greetings = [(first, start), (start, first), (end, first)]
        for other in others:
            greetings += [(other, start), (other, first)]
        for source, target in greetings:
            signal(p == source, barrier, {"prop": target})
            neighbours += (p == target).astype(jnp.int32)

    interior = slice(LANES, LANES + size)
    loads = [
        pltpu.make_async_copy(field_hbm, x.at[:, :, :, interior], local_sem.at[0]),
        pltpu.make_async_copy(rhs_hbm, rhs, local_sem.at[1]),
        pltpu.make_async_copy(eps_hbm, eps, local_sem.at[2]),
        pltpu.make_async_copy(cells_hbm, cells, local_sem.at[3]),
        pltpu.make_async_copy(profile_hbm, profile, local_sem.at[4]),
    ]
    for load in loads:
        load.start()

    pl.semaphore_wait(barrier, neighbours)
    for start, end, (first, *others) in sides:
        for one in (start, *others):
            signal(p == first, far_sem, {"prop": one})

    def lanes(c):
        return slice(c * chunk, (c + 1) * chunk)

    def down_parts(sweep, c):
        src = field_hbm.at[:, 0:2, :, lanes(c)] if sweep == 0 else p_own.at[:, :, :, lanes(c)]
        dst = (e_next, p_next)[sweep].at[:, :, :, lanes(c)]
        return src, dst, down_send.at[sweep, c], down_recv.at[sweep, c]

    def down(sweep, c):
        return remote(*down_parts(sweep, c), below)

    def up_parts(sweep, c):
        src = field_hbm.at[:, 3:5, :, lanes(c)] if sweep == 0 else q_own.at[:, :, :, lanes(c)]
        dst = (h_prev, q_prev)[sweep].at[:, :, :, lanes(c)]
        return src, dst, up_send.at[sweep, c], up_recv.at[sweep, c]

    def up(sweep, c):
        return remote(*up_parts(sweep, c), above)

    eps_copy = remote(eps_hbm, eps_next, eps_sem.at[0], eps_sem.at[1], below)

    def to_pass(sweep, c, i, is_up, by):
        src, _, send, _ = (up_parts if is_up else down_parts)(sweep, c)
        return remote(src, passing.at[sweep, i], send, pass_recv.at[sweep, i], {"prop": by})

    def pass_on(sweep, c, i, is_up):
        _, dst, _, recv = (up_parts if is_up else down_parts)(sweep, c)
        end = LAST + 1 if is_up else LAST
        return remote(passing.at[sweep, i], dst, pass_send.at[sweep, i], recv, {"prop": end})

    def start_pass(sweep):
        for at, c, way, i in RELAYED:
            if at == sweep:
                for is_up, start, by in ((True, LAST, UP_BY[way - 1]), (False, LAST + 1, DOWN_BY[way - 1])):

                    @pl.when(p == start)
                    def _():
                        to_pass(sweep, c, i, is_up, by).start()

    def start_near(sweep):
        for c in range(CHUNKS):

            @pl.when(near_below)
            def _():
                down(sweep, c).start()

            @pl.when(near_above)
            def _():
                up(sweep, c).start()

    def start_far(sweep):
        for c in range(CHUNKS):
            if WAYS[sweep][c] == 0:

                @pl.when(p == LAST + 1)
                def _():
                    down(sweep, c).start()

                @pl.when(p == LAST)
                def _():
                    up(sweep, c).start()

    def pass_all(sweep):
        for at, c, way, i in RELAYED:
            if at == sweep:
                for is_up, by in ((True, UP_BY[way - 1]), (False, DOWN_BY[way - 1])):

                    @pl.when(p == by)
                    def _():
                        to_pass(sweep, c, i, is_up, by).wait_recv()
                        pass_on(sweep, c, i, is_up).start()

    start_pass(0)
    start_near(0)

    @pl.when(near_below)
    def _():
        eps_copy.start()

    def to_low(sweep):
        return remote(
            low_out.at[sweep], high_in.at[sweep], edge_send.at[sweep, 0], edge_recv.at[sweep, 0],
            {"harm": h - 1},
        )

    def to_high(sweep):
        return remote(
            high_out.at[sweep], low_in.at[sweep], edge_send.at[sweep, 1], edge_recv.at[sweep, 1],
            {"harm": h + 1},
        )

    def send_edges(sweep, fields):
        for c in range(2):
            for k in range(3):
                i = c * 3 + k
                low_out[sweep, i : i + 1, :] = fields[c, k, 0:1, interior]
                high_out[sweep, i : i + 1, :] = fields[c, k, 7:8, interior]

        @pl.when(has_low)
        def _():
            to_low(sweep).start()

        @pl.when(has_high)
        def _():
            to_high(sweep).start()

    def wait_edges(sweep):
        @pl.when(has_high)
        def _():
            to_low(sweep).wait_recv()

        @pl.when(has_low)
        def _():
            to_high(sweep).wait_recv()

    for sweep in range(2):
        low_out[sweep, 6:8, :] = jnp.zeros((2, size), jnp.float32)
        high_out[sweep, 6:8, :] = jnp.zeros((2, size), jnp.float32)
    loads[0].wait()
    send_edges(0, x)

    @pl.when(jnp.logical_not(has_low))
    def _():
        low_in[...] = jnp.zeros_like(low_in)

    @pl.when(jnp.logical_not(has_high))
    def _():
        high_in[...] = jnp.zeros_like(high_in)

    @pl.when(jnp.logical_not(has_below))
    def _():
        h_prev[...] = jnp.zeros_like(h_prev)
        q_prev[...] = jnp.zeros_like(q_prev)

    @pl.when(jnp.logical_not(has_above))
    def _():
        e_next[...] = jnp.zeros_like(e_next)
        p_next[...] = jnp.zeros_like(p_next)
        eps_next[...] = jnp.ones_like(eps_next)

    pad = jnp.zeros((2, 3, 8, LANES), jnp.float32)
    for fields in (x, y):
        fields[:, 0:3, :, LANES + size :] = pad
        fields[:, 3:6, :, :LANES] = pad

    harmonic = h * 8 + lax.broadcasted_iota(jnp.int32, (8, 1), 0)
    omega = BASE_FREQUENCY + MOD_FREQUENCY * (harmonic - HARMONICS // 2).astype(jnp.float32)
    a = 1.0 / omega
    for load in loads[2:]:
        load.wait()
    dense = mod_tables(p.astype(jnp.float32), cells[...], profile[...], count, amp, phase)
    for i in range(size // LANES):
        part = slice(i * LANES, (i + 1) * LANES)
        inverse = 1.0 / eps[:, part]
        tab[0, :, part] = jnp.broadcast_to(dense[i : i + 1, :] * inverse, (8, LANES))
        tab[1, :, part] = jnp.broadcast_to(dense[PROFILES + i : PROFILES + i + 1, :] * inverse, (8, LANES))
        tab[2, :, part] = a * inverse
    loads[1].wait()

    told = [one for start, end, (first, *others) in sides for one in (start, *others)]

    @pl.when(functools.reduce(jnp.logical_or, [p == one for one in told]))
    def _():
        pl.semaphore_wait(far_sem, 1)

    start_far(0)

    @pl.when(p == LAST + 1)
    def _():
        eps_copy.start()

    pass_all(0)
    wait_edges(0)

    def to_first(k, c, here, value):
        if k in (0, 1):
            p_own[c, k, :, here] = value
        elif k in (3, 4):
            q_own[c, k - 3, :, here] = value
        else:
            y[c, k, :, pl.ds(pl.multiple_of(here.start + LANES, LANES), here.size)] = value

    partial_sweep(x, rhs, low_in.at[0], high_in.at[0], tab, a, to_first, size)
    start_pass(1)
    start_near(1)
    start_far(1)
    pass_all(1)

    for c in range(CHUNKS):

        @pl.when(has_above)
        def _():
            down(0, c).wait_recv()

        @pl.when(has_below)
        def _():
            up(0, c).wait_recv()

        part = lanes(c)
        wide = slice(LANES + c * chunk, LANES + (c + 1) * chunk)
        ae = tab[2, :, part]
        for i in range(2):
            s = 1.0 if i == 1 else -1.0
            y[1 - i, 0, :, wide] = p_own[1 - i, 0, :, part] + s * ae * h_prev[i, 1, :, part]
            y[1 - i, 1, :, wide] = p_own[1 - i, 1, :, part] - s * ae * h_prev[i, 0, :, part]
            y[1 - i, 3, :, wide] = q_own[1 - i, 0, :, part] + s * a * e_next[i, 1, :, part]
            y[1 - i, 4, :, wide] = q_own[1 - i, 1, :, part] - s * a * e_next[i, 0, :, part]

    send_edges(1, y)

    @pl.when(has_above)
    def _():
        eps_copy.wait_recv()

    above_factor = has_above.astype(jnp.float32)
    below_factor = has_below.astype(jnp.float32)
    wait_edges(1)

    def to_second(k, c, here, value):
        res[c, k, :, here] = value

    partial_sweep(y, rhs, low_in.at[1], high_in.at[1], tab, a, to_second, size)
    outs = [
        pltpu.make_async_copy(res.at[:, k], out_hbm.at[:, k], out_sem.at[0, i])
        for i, k in enumerate((2, 5))
    ]
    for copy in outs:
        copy.start()

    for c in range(CHUNKS):
        part = lanes(c)
        wide = slice(LANES + c * chunk, LANES + (c + 1) * chunk)

        @pl.when(has_above)
        def _():
            down(1, c).wait_recv()

        @pl.when(has_below)
        def _():
            up(1, c).wait_recv()

        ae = tab[2, :, part]
        ae_next = a * (above_factor / eps_next[:, part])
        a_below = a * below_factor
        for i in range(2):
            s = 1.0 if i == 1 else -1.0
            j = 1 - i
            ex = p_next[i, 0, :, part] - s * ae_next * x[j, 4, :, wide]
            ey = p_next[i, 1, :, part] + s * ae_next * x[j, 3, :, wide]
            hx = q_prev[i, 0, :, part] - s * a_below * x[j, 1, :, wide]
            hy = q_prev[i, 1, :, part] + s * a_below * x[j, 0, :, wide]
            res[j, 0, :, part] += s * ae * hy
            res[j, 1, :, part] -= s * ae * hx
            res[j, 3, :, part] += s * a * ey
            res[j, 4, :, part] -= s * a * ex
        for i, k in enumerate((0, 3)):
            copy = pltpu.make_async_copy(
                res.at[:, k : k + 2, :, part], out_hbm.at[:, k : k + 2, :, part], out_sem.at[c + 1, i]
            )
            copy.start()
            outs.append(copy)

    @pl.when(has_below)
    def _():
        eps_copy.wait_send()

    for sweep in range(2):

        @pl.when(has_low)
        def _():
            to_low(sweep).wait_send()

        @pl.when(has_high)
        def _():
            to_high(sweep).wait_send()

        for c in range(CHUNKS):

            @pl.when(has_below)
            def _():
                down(sweep, c).wait_send()

            @pl.when(has_above)
            def _():
                up(sweep, c).wait_send()

    for sweep, c, way, i in RELAYED:
        for is_up, by in ((True, UP_BY[way - 1]), (False, DOWN_BY[way - 1])):

            @pl.when(p == by)
            def _():
                pass_on(sweep, c, i, is_up).wait_send()

    for copy in outs:
        copy.wait()


def local(rhs_field, field_guess, permittivity, mod_cells, mod_count, mod_profile, mod_amp, mod_phase):
    size = permittivity.shape[0]
    listed = mod_cells.shape[1]
    f32 = jnp.float32
    whole = (2, 6, 8, size)
    padded = (2, 6, 8, size + 2 * LANES)
    face = (2, 2, 8, size)
    dma = pltpu.SemaphoreType.DMA
    anywhere, smem = pl.BlockSpec(memory_space=pl.ANY), pl.BlockSpec(memory_space=pltpu.SMEM)
    return pl.pallas_call(
        kernel,
        out_shape=jax.ShapeDtypeStruct(whole, f32),
        in_specs=[anywhere] * 5 + [smem] * 3,
        out_specs=anywhere,
        scratch_shapes=[
            pltpu.VMEM(padded, f32), pltpu.VMEM(padded, f32), pltpu.VMEM(whole, f32), pltpu.VMEM(whole, f32),
            *[pltpu.VMEM(face, f32)] * 6,
            pltpu.VMEM((1, size), f32), pltpu.VMEM((1, size), f32),
            pltpu.VMEM((1, listed), jnp.int32), pltpu.VMEM((1, listed), jnp.int32),
            pltpu.VMEM((3, 8, size), f32),
            *[pltpu.VMEM((2, 8, size), f32)] * 4,
            pltpu.SemaphoreType.REGULAR, pltpu.VMEM((2, SLOTS, 2, 2, 8, size // CHUNKS), f32), dma((2, SLOTS)), dma((2, SLOTS)),
            dma((5,)), dma((CHUNKS + 1, 2)), dma((2,)), dma((2, 2)), dma((2, 2)),
            *[dma((2, CHUNKS))] * 4,
        ],
        compiler_params=pltpu.CompilerParams(
            collective_id=0, has_side_effects=True, vmem_limit_bytes=60 * 2**20
        ),
        name="sweeps",
    )(rhs_field, field_guess, permittivity.reshape(1, size), mod_cells, mod_profile, mod_count, mod_amp, mod_phase)


def solution(mesh):
    return jax.shard_map(
        local,
        mesh=mesh,
        in_specs=(
            P(None, None, "harm", "prop"),
            P(None, None, "harm", "prop"),
            P("prop"),
            P("prop", None),
            P("prop"),
            P("prop", None),
            P(),
            P(),
        ),
        out_specs=P(None, None, "harm", "prop"),
        check_vma=False,
    )
```

```python
import functools

import jax
import jax.numpy as jnp
from jax import lax
from jax.experimental import pallas as pl
from jax.experimental.pallas import tpu as pltpu
from jax.sharding import PartitionSpec as P

HARMONICS = 64
TX = 64
BASE_FREQUENCY = 6.0
MOD_FREQUENCY = 0.05
WAVE_NUMBER = 0.3
PROFILES = 16
MESH = pl.DeviceIdType.MESH
LANES = 128
BLOCK = 512
CHUNKS = 8
LAST = 15
UP_WAYS = ((0, 12, 3, None, 0, 12, 3, None), (0, 12, 3, None, 0, 12, None, None))
DOWN_WAYS = ((19, 28, 24, None, 19, 28, 24, None), (19, 28, 24, None, 19, 28, None, None))
UP_FIRST, DOWN_FIRST = (0, 19)
RELAYED = [
    (sweep, c, is_up, by, ways[sweep][:c].count(by))
    for is_up, ways in ((True, UP_WAYS), (False, DOWN_WAYS))
    for sweep in range(2)
    for c, by in enumerate(ways[sweep])
    if by is not None
]
SLOTS = 1 + max(i for *_, i in RELAYED)


def remote(src, dst, send, recv, device):
    return pltpu.make_async_remote_copy(
        src_ref=src, dst_ref=dst, send_sem=send, recv_sem=recv, device_id=device, device_id_type=MESH
    )


def signal(condition, sem, device):
    @pl.when(condition)
    def _():
        pl.semaphore_signal(sem, inc=1, device_id=device, device_id_type=MESH)


def mod_tables(plane, cells, profile, count, amp, phase):
    row = lax.broadcasted_iota(jnp.int32, (PROFILES, LANES), 0)
    amps = jnp.zeros((PROFILES, LANES), jnp.float32)
    phases = jnp.zeros((PROFILES, LANES), jnp.float32)
    for i in range(PROFILES):
        amps = jnp.where(row == i, amp[i], amps)
        phases = jnp.where(row == i, phase[i], phases)
    angle = phases - WAVE_NUMBER * plane
    cosines = 0.5 * amps * jnp.cos(angle)
    sines = 0.5 * amps * jnp.sin(angle)
    length = cells.shape[1]
    live = count[0]
    lane = lax.broadcasted_iota(jnp.int32, (1, LANES), 1)
    low_row = lax.broadcasted_iota(jnp.int32, (LANES, LANES), 0)
    left, right = [], []
    for j in range(length // LANES):
        part = slice(j * LANES, (j + 1) * LANES)
        cell, prof = cells[:, part], profile[:, part]
        active = (lane + j * LANES) < live
        here = (row == cell // LANES) & active
        hit = row == prof
        cosine = jnp.sum(jnp.where(hit, cosines, 0.0), axis=0, keepdims=True)
        sine = jnp.sum(jnp.where(hit, sines, 0.0), axis=0, keepdims=True)
        left.append(
            jnp.concatenate([jnp.where(here, cosine, 0.0), jnp.where(here, sine, 0.0)], axis=0)
        )
        right.append((low_row == cell % LANES).astype(jnp.float32))
    return lax.dot_general(
        jnp.concatenate(left, axis=1),
        jnp.concatenate(right, axis=1),
        (((1,), (1,)), ((), ())),
        precision=lax.Precision.HIGHEST,
        preferred_element_type=jnp.float32,
    )


def partial_sweep(fields, rhs, low_edge, high_edge, tab, a, out, cells, electric, magnetic):
    width = min(BLOCK, cells)
    wide = width + LANES
    lane = lax.broadcasted_iota(jnp.int32, (8, width), 1)
    column = lane % TX
    not_last, not_first = column != TX - 1, column != 0
    row = lax.broadcasted_iota(jnp.int32, (8, width), 0)

    def body(step, carry):
        at = pl.multiple_of(step * width, LANES)
        here = pl.ds(at, width)
        mid = pl.ds(pl.multiple_of(at + LANES, LANES), width)

        def ahead(c, k):
            v = fields[c, k, :, pl.ds(pl.multiple_of(at + LANES, LANES), wide)]
            own = v[:, :width]
            dy = pltpu.roll(v, wide - TX, 1)[:, :width] - own
            dx = jnp.where(not_last, pltpu.roll(v, wide - 1, 1)[:, :width], 0.0) - own
            return own, dy, dx

        def behind(c, k):
            v = fields[c, k, :, pl.ds(at, wide)]
            own = v[:, LANES:]
            dy = own - pltpu.roll(v, TX, 1)[:, LANES:]
            dx = own - jnp.where(not_first, pltpu.roll(v, 1, 1)[:, LANES:], 0.0)
            return own, dy, dx

        if electric:
            cos_t, sin_t, ae = (tab[i, :, here] for i in range(3))
        couple = []
        for k in range(3 if electric else 0):
            low, high = [], []
            for c in range(2):
                v = fields[c, k, :, mid]
                i = c * 3 + k
                first = 0.0 if low_edge is None else low_edge[i : i + 1, here]
                last = 0.0 if high_edge is None else high_edge[i : i + 1, here]
                low.append(jnp.where(row == 0, first, pltpu.roll(v, 1, 0)))
                high.append(jnp.where(row == 7, last, pltpu.roll(v, 7, 0)))
            couple.append(
                (
                    cos_t * (low[0] + high[0]) + sin_t * (high[1] - low[1]),
                    cos_t * (low[1] + high[1]) + sin_t * (low[0] - high[0]),
                )
            )
        for c in range(2):
            s = 1.0 if c == 1 else -1.0
            if magnetic:
                ex, ex_y, _ = ahead(c, 0)
                ey, _, ey_x = ahead(c, 1)
                _, ez_y, ez_x = ahead(c, 2)
                sa = s * a
                out(3, 1 - c, here, sa * (rhs[c, 3, :, here] - ez_y - ey))
                out(4, 1 - c, here, sa * (rhs[c, 4, :, here] + ex + ez_x))
                out(5, 1 - c, here, sa * (rhs[c, 5, :, here] - ey_x + ex_y))
            if electric:
                hx, hx_y, _ = behind(c, 3)
                hy, _, hy_x = behind(c, 4)
                _, hz_y, hz_x = behind(c, 5)
                sae = s * ae
                out(0, 1 - c, here, sae * (rhs[c, 0, :, here] + hz_y - hy) - couple[0][1 - c])
                out(1, 1 - c, here, sae * (rhs[c, 1, :, here] + hx - hz_x) - couple[1][1 - c])
                out(2, 1 - c, here, sae * (rhs[c, 2, :, here] + hy_x - hx_y) - couple[2][1 - c])
        return carry

    lax.fori_loop(0, cells // width, body, 0)


def add_edges(low_edge, high_edge, tab, res, cells):
    width = min(BLOCK, cells)
    row = lax.broadcasted_iota(jnp.int32, (8, width), 0)

    def body(step, carry):
        here = pl.ds(pl.multiple_of(step * width, LANES), width)
        cos_t, sin_t = tab[0, :, here], tab[1, :, here]
        for k in range(3):
            low_re, low_im, high_re, high_im = (
                jnp.where(row == at, edge[i : i + 1, here], 0.0)
                for at, edge, i in ((0, low_edge, k), (0, low_edge, 3 + k), (7, high_edge, k), (7, high_edge, 3 + k))
            )
            res[0, k, :, here] -= cos_t * (low_re + high_re) + sin_t * (high_im - low_im)
            res[1, k, :, here] -= cos_t * (low_im + high_im) + sin_t * (low_re - high_re)
        return carry

    lax.fori_loop(0, cells // width, body, 0)


def kernel(
    rhs_hbm, field_hbm, eps_hbm, cells_hbm, profile_hbm, count, amp, phase, out_hbm,
    x, y, rhs, res, p_own, q_own, e_next, h_prev, p_next, q_prev, eps, eps_next, cells, profile,
    tab, low_out, high_out, low_in, high_in,
    far_sem, passing, pass_recv, pass_send, local_sem, out_sem, eps_sem, edge_send, edge_recv, down_send, down_recv, up_send, up_recv,
):
    h, p = lax.axis_index("harm"), lax.axis_index("prop")
    nh, np_ = lax.axis_size("harm"), lax.axis_size("prop")
    size = rhs.shape[3]
    chunk = size // CHUNKS
    below, above = {"prop": p - 1}, {"prop": p + 1}
    has_below, has_above = p > 0, p < np_ - 1
    has_low, has_high = h > 0, h < nh - 1

    near_above, near_below = has_above & (p != LAST), has_below & (p != LAST + 1)
    sides = [
        (LAST, LAST + 1, [UP_FIRST] + sorted({by for *_, is_up, by, _ in RELAYED if is_up} - {UP_FIRST})),
        (LAST + 1, LAST, [DOWN_FIRST] + sorted({by for *_, is_up, by, _ in RELAYED if not is_up} - {DOWN_FIRST})),
    ]
    barrier = pltpu.get_barrier_semaphore()
    signal(near_below, barrier, below)
    signal(near_above, barrier, above)
    signal(has_low, barrier, {"harm": h - 1})
    signal(has_high, barrier, {"harm": h + 1})
    neighbours = sum(
        condition.astype(jnp.int32) for condition in (near_below, near_above, has_low, has_high)
    )
    for start, end, (first, *others) in sides:
        greetings = [(first, start), (start, first), (end, first)]
        for other in others:
            greetings += [(other, start), (other, first)]
        for source, target in greetings:
            signal(p == source, barrier, {"prop": target})
            neighbours += (p == target).astype(jnp.int32)

    interior = slice(LANES, LANES + size)
    loads = [
        pltpu.make_async_copy(field_hbm, x.at[:, :, :, interior], local_sem.at[0]),
        pltpu.make_async_copy(rhs_hbm, rhs, local_sem.at[1]),
        pltpu.make_async_copy(eps_hbm, eps, local_sem.at[2]),
        pltpu.make_async_copy(cells_hbm, cells, local_sem.at[3]),
        pltpu.make_async_copy(profile_hbm, profile, local_sem.at[4]),
    ]
    for load in loads:
        load.start()

    def pack_edges(sweep, fields):
        for c in range(2):
            for k in range(3):
                i = c * 3 + k
                low_out[sweep, i : i + 1, :] = fields[c, k, 0:1, interior]
                high_out[sweep, i : i + 1, :] = fields[c, k, 7:8, interior]

    for sweep in range(2):
        low_out[sweep, 6:8, :] = jnp.zeros((2, size), jnp.float32)
        high_out[sweep, 6:8, :] = jnp.zeros((2, size), jnp.float32)
    loads[0].wait()
    pack_edges(0, x)

    @pl.when(jnp.logical_not(has_low))
    def _():
        low_in[...] = jnp.zeros_like(low_in)

    @pl.when(jnp.logical_not(has_high))
    def _():
        high_in[...] = jnp.zeros_like(high_in)

    @pl.when(jnp.logical_not(has_below))
    def _():
        h_prev[...] = jnp.zeros_like(h_prev)
        q_prev[...] = jnp.zeros_like(q_prev)

    @pl.when(jnp.logical_not(has_above))
    def _():
        e_next[...] = jnp.zeros_like(e_next)
        p_next[...] = jnp.zeros_like(p_next)
        eps_next[...] = jnp.ones_like(eps_next)

    pad = jnp.zeros((2, 3, 8, LANES), jnp.float32)
    for fields in (x, y):
        fields[:, 0:3, :, LANES + size :] = pad
        fields[:, 3:6, :, :LANES] = pad

    harmonic = h * 8 + lax.broadcasted_iota(jnp.int32, (8, 1), 0)
    omega = BASE_FREQUENCY + MOD_FREQUENCY * (harmonic - HARMONICS // 2).astype(jnp.float32)
    a = 1.0 / omega
    loads[1].wait()

    def to_first(k, c, here, value):
        if k in (0, 1):
            p_own[c, k, :, here] = value
        elif k in (3, 4):
            q_own[c, k - 3, :, here] = value
        else:
            y[c, k, :, pl.ds(pl.multiple_of(here.start + LANES, LANES), here.size)] = value

    partial_sweep(x, rhs, None, None, tab, a, to_first, size, False, True)
    pl.semaphore_wait(barrier, neighbours)
    for start, end, (first, *others) in sides:
        for one in (start, *others):
            signal(p == first, far_sem, {"prop": one})

    def lanes(c):
        return slice(c * chunk, (c + 1) * chunk)

    def down_parts(sweep, c):
        src = field_hbm.at[:, 0:2, :, lanes(c)] if sweep == 0 else p_own.at[:, :, :, lanes(c)]
        dst = (e_next, p_next)[sweep].at[:, :, :, lanes(c)]
        return src, dst, down_send.at[sweep, c], down_recv.at[sweep, c]

    def down(sweep, c):
        return remote(*down_parts(sweep, c), below)

    def up_parts(sweep, c):
        src = field_hbm.at[:, 3:5, :, lanes(c)] if sweep == 0 else q_own.at[:, :, :, lanes(c)]
        dst = (h_prev, q_prev)[sweep].at[:, :, :, lanes(c)]
        return src, dst, up_send.at[sweep, c], up_recv.at[sweep, c]

    def up(sweep, c):
        return remote(*up_parts(sweep, c), above)

    eps_copy = remote(eps_hbm, eps_next, eps_sem.at[0], eps_sem.at[1], below)

    def to_pass(sweep, c, i, is_up, by):
        src, _, send, _ = (up_parts if is_up else down_parts)(sweep, c)
        return remote(src, passing.at[sweep, i], send, pass_recv.at[sweep, i], {"prop": by})

    def pass_on(sweep, c, i, is_up):
        _, dst, _, recv = (up_parts if is_up else down_parts)(sweep, c)
        end = LAST + 1 if is_up else LAST
        return remote(passing.at[sweep, i], dst, pass_send.at[sweep, i], recv, {"prop": end})

    def start_pass(sweep, upward):
        for at, c, is_up, by, i in RELAYED:
            if at == sweep and is_up == upward:

                @pl.when(p == (LAST if is_up else LAST + 1))
                def _():
                    to_pass(sweep, c, i, is_up, by).start()

    def start_near(sweep, upward):
        for c in range(CHUNKS):

            @pl.when(near_above if upward else near_below)
            def _():
                (up if upward else down)(sweep, c).start()

    def start_far(sweep, upward):
        for c in range(CHUNKS):
            if (UP_WAYS if upward else DOWN_WAYS)[sweep][c] is None:

                @pl.when(p == (LAST if upward else LAST + 1))
                def _():
                    (up if upward else down)(sweep, c).start()

    def pass_all(sweep, by_first):
        for at, c, is_up, by, i in RELAYED:
            if at == sweep and by_first == (by in (UP_FIRST, DOWN_FIRST)):

                @pl.when(p == by)
                def _():
                    to_pass(sweep, c, i, is_up, by).wait_recv()
                    pass_on(sweep, c, i, is_up).start()

    def wait_far(slabs):
        @pl.when(functools.reduce(jnp.logical_or, [p == one for one in slabs]))
        def _():
            pl.semaphore_wait(far_sem, 1)

    def to_low(sweep):
        return remote(
            low_out.at[sweep], high_in.at[sweep], edge_send.at[sweep, 0], edge_recv.at[sweep, 0],
            {"harm": h - 1},
        )

    def to_high(sweep):
        return remote(
            high_out.at[sweep], low_in.at[sweep], edge_send.at[sweep, 1], edge_recv.at[sweep, 1],
            {"harm": h + 1},
        )

    def send_edges(sweep):
        @pl.when(has_low)
        def _():
            to_low(sweep).start()

        @pl.when(has_high)
        def _():
            to_high(sweep).start()

    def wait_edges(sweep):
        @pl.when(has_high)
        def _():
            to_low(sweep).wait_recv()

        @pl.when(has_low)
        def _():
            to_high(sweep).wait_recv()

    send_edges(0)
    for upward in (True, False):
        start_pass(0, upward)
    start_pass(1, True)
    for upward in (True, False):
        start_near(0, upward)
    start_near(1, True)

    @pl.when(near_below)
    def _():
        eps_copy.start()

    for load in loads[2:]:
        load.wait()
    dense = mod_tables(p.astype(jnp.float32), cells[...], profile[...], count, amp, phase)
    for i in range(size // LANES):
        part = slice(i * LANES, (i + 1) * LANES)
        inverse = 1.0 / eps[:, part]
        tab[0, :, part] = jnp.broadcast_to(dense[i : i + 1, :] * inverse, (8, LANES))
        tab[1, :, part] = jnp.broadcast_to(dense[PROFILES + i : PROFILES + i + 1, :] * inverse, (8, LANES))
        tab[2, :, part] = a * inverse

    wait_far((LAST, LAST + 1))
    for upward in (True, False):
        start_far(0, upward)
    start_far(1, True)

    @pl.when(p == LAST + 1)
    def _():
        eps_copy.start()

    pass_all(0, True)
    wait_edges(0)

    partial_sweep(x, rhs, low_in.at[0], high_in.at[0], tab, a, to_first, size, True, False)
    start_pass(1, False)
    start_near(1, False)
    wait_far([one for _, _, (_, *others) in sides for one in others])
    start_far(1, False)
    pass_all(0, False)
    pass_all(1, True)
    pass_all(1, False)

    for c in range(CHUNKS):

        @pl.when(has_above)
        def _():
            down(0, c).wait_recv()

        @pl.when(has_below)
        def _():
            up(0, c).wait_recv()

        part = lanes(c)
        wide = slice(LANES + c * chunk, LANES + (c + 1) * chunk)
        ae = tab[2, :, part]
        for i in range(2):
            s = 1.0 if i == 1 else -1.0
            y[1 - i, 0, :, wide] = p_own[1 - i, 0, :, part] + s * ae * h_prev[i, 1, :, part]
            y[1 - i, 1, :, wide] = p_own[1 - i, 1, :, part] - s * ae * h_prev[i, 0, :, part]
            y[1 - i, 3, :, wide] = q_own[1 - i, 0, :, part] + s * a * e_next[i, 1, :, part]
            y[1 - i, 4, :, wide] = q_own[1 - i, 1, :, part] - s * a * e_next[i, 0, :, part]

    pack_edges(1, y)
    send_edges(1)

    @pl.when(has_above)
    def _():
        eps_copy.wait_recv()

    above_factor = has_above.astype(jnp.float32)
    below_factor = has_below.astype(jnp.float32)

    def to_second(k, c, here, value):
        res[c, k, :, here] = value

    partial_sweep(y, rhs, None, None, tab, a, to_second, size, True, True)
    wait_edges(1)
    add_edges(low_in.at[1], high_in.at[1], tab, res, size)
    outs = [
        pltpu.make_async_copy(res.at[:, k], out_hbm.at[:, k], out_sem.at[0, i])
        for i, k in enumerate((2, 5))
    ]
    for copy in outs:
        copy.start()

    for c in range(CHUNKS):
        part = lanes(c)
        wide = slice(LANES + c * chunk, LANES + (c + 1) * chunk)

        @pl.when(has_above)
        def _():
            down(1, c).wait_recv()

        @pl.when(has_below)
        def _():
            up(1, c).wait_recv()

        ae = tab[2, :, part]
        ae_next = a * (above_factor / eps_next[:, part])
        a_below = a * below_factor
        for i in range(2):
            s = 1.0 if i == 1 else -1.0
            j = 1 - i
            ex = p_next[i, 0, :, part] - s * ae_next * x[j, 4, :, wide]
            ey = p_next[i, 1, :, part] + s * ae_next * x[j, 3, :, wide]
            hx = q_prev[i, 0, :, part] - s * a_below * x[j, 1, :, wide]
            hy = q_prev[i, 1, :, part] + s * a_below * x[j, 0, :, wide]
            res[j, 0, :, part] += s * ae * hy
            res[j, 1, :, part] -= s * ae * hx
            res[j, 3, :, part] += s * a * ey
            res[j, 4, :, part] -= s * a * ex
        for i, k in enumerate((0, 3)):
            copy = pltpu.make_async_copy(
                res.at[:, k : k + 2, :, part], out_hbm.at[:, k : k + 2, :, part], out_sem.at[c + 1, i]
            )
            copy.start()
            outs.append(copy)

    @pl.when(has_below)
    def _():
        eps_copy.wait_send()

    for sweep in range(2):

        @pl.when(has_low)
        def _():
            to_low(sweep).wait_send()

        @pl.when(has_high)
        def _():
            to_high(sweep).wait_send()

        for c in range(CHUNKS):

            @pl.when(has_below)
            def _():
                down(sweep, c).wait_send()

            @pl.when(has_above)
            def _():
                up(sweep, c).wait_send()

    for sweep, c, is_up, by, i in RELAYED:

        @pl.when(p == by)
        def _():
            pass_on(sweep, c, i, is_up).wait_send()

    for copy in outs:
        copy.wait()


def local(rhs_field, field_guess, permittivity, mod_cells, mod_count, mod_profile, mod_amp, mod_phase):
    size = permittivity.shape[0]
    listed = mod_cells.shape[1]
    f32 = jnp.float32
    whole = (2, 6, 8, size)
    padded = (2, 6, 8, size + 2 * LANES)
    face = (2, 2, 8, size)
    dma = pltpu.SemaphoreType.DMA
    anywhere, smem = pl.BlockSpec(memory_space=pl.ANY), pl.BlockSpec(memory_space=pltpu.SMEM)
    return pl.pallas_call(
        kernel,
        out_shape=jax.ShapeDtypeStruct(whole, f32),
        in_specs=[anywhere] * 5 + [smem] * 3,
        out_specs=anywhere,
        scratch_shapes=[
            pltpu.VMEM(padded, f32), pltpu.VMEM(padded, f32), pltpu.VMEM(whole, f32), pltpu.VMEM(whole, f32),
            *[pltpu.VMEM(face, f32)] * 6,
            pltpu.VMEM((1, size), f32), pltpu.VMEM((1, size), f32),
            pltpu.VMEM((1, listed), jnp.int32), pltpu.VMEM((1, listed), jnp.int32),
            pltpu.VMEM((3, 8, size), f32),
            *[pltpu.VMEM((2, 8, size), f32)] * 4,
            pltpu.SemaphoreType.REGULAR, pltpu.VMEM((2, SLOTS, 2, 2, 8, size // CHUNKS), f32), dma((2, SLOTS)), dma((2, SLOTS)),
            dma((5,)), dma((CHUNKS + 1, 2)), dma((2,)), dma((2, 2)), dma((2, 2)),
            *[dma((2, CHUNKS))] * 4,
        ],
        compiler_params=pltpu.CompilerParams(
            collective_id=0, has_side_effects=True, vmem_limit_bytes=60 * 2**20
        ),
        name="sweeps",
    )(rhs_field, field_guess, permittivity.reshape(1, size), mod_cells, mod_profile, mod_count, mod_amp, mod_phase)


def solution(mesh):
    return jax.shard_map(
        local,
        mesh=mesh,
        in_specs=(
            P(None, None, "harm", "prop"),
            P(None, None, "harm", "prop"),
            P("prop"),
            P("prop", None),
            P("prop"),
            P("prop", None),
            P(),
            P(),
        ),
        out_specs=P(None, None, "harm", "prop"),
        check_vma=False,
    )
```

```python
import functools

import jax
import jax.numpy as jnp
from jax import lax
from jax.experimental import pallas as pl
from jax.experimental.pallas import tpu as pltpu
from jax.sharding import PartitionSpec as P

HARMONICS = 64
TX = 64
BASE_FREQUENCY = 6.0
MOD_FREQUENCY = 0.05
WAVE_NUMBER = 0.3
PROFILES = 16
MESH = pl.DeviceIdType.MESH
LANES = 128
BLOCK = 512
CHUNKS = 8
LAST = 15
UP_WAYS = ((0, 12, 3, None, 0, 12, 3, 0), (12, 0, None, 3, 12, None, None, None))
DOWN_WAYS = ((19, 28, 24, None, 19, 28, 24, None), (19, 28, 24, None, 19, 28, None, None))
UP_FIRST, DOWN_FIRST = (0, 19)
RELAYED = [
    (sweep, c, is_up, by, ways[sweep][:c].count(by))
    for is_up, ways in ((True, UP_WAYS), (False, DOWN_WAYS))
    for sweep in range(2)
    for c, by in enumerate(ways[sweep])
    if by is not None
]
SLOTS = 1 + max(i for *_, i in RELAYED)


def remote(src, dst, send, recv, device):
    return pltpu.make_async_remote_copy(
        src_ref=src, dst_ref=dst, send_sem=send, recv_sem=recv, device_id=device, device_id_type=MESH
    )


def signal(condition, sem, device):
    @pl.when(condition)
    def _():
        pl.semaphore_signal(sem, inc=1, device_id=device, device_id_type=MESH)


def mod_tables(plane, cells, profile, count, amp, phase):
    row = lax.broadcasted_iota(jnp.int32, (PROFILES, LANES), 0)
    amps = jnp.zeros((PROFILES, LANES), jnp.float32)
    phases = jnp.zeros((PROFILES, LANES), jnp.float32)
    for i in range(PROFILES):
        amps = jnp.where(row == i, amp[i], amps)
        phases = jnp.where(row == i, phase[i], phases)
    angle = phases - WAVE_NUMBER * plane
    cosines = 0.5 * amps * jnp.cos(angle)
    sines = 0.5 * amps * jnp.sin(angle)
    length = cells.shape[1]
    live = count[0]
    lane = lax.broadcasted_iota(jnp.int32, (1, LANES), 1)
    low_row = lax.broadcasted_iota(jnp.int32, (LANES, LANES), 0)
    left, right = [], []
    for j in range(length // LANES):
        part = slice(j * LANES, (j + 1) * LANES)
        cell, prof = cells[:, part], profile[:, part]
        active = (lane + j * LANES) < live
        here = (row == cell // LANES) & active
        hit = row == prof
        cosine = jnp.sum(jnp.where(hit, cosines, 0.0), axis=0, keepdims=True)
        sine = jnp.sum(jnp.where(hit, sines, 0.0), axis=0, keepdims=True)
        left.append(
            jnp.concatenate([jnp.where(here, cosine, 0.0), jnp.where(here, sine, 0.0)], axis=0)
        )
        right.append((low_row == cell % LANES).astype(jnp.float32))
    return lax.dot_general(
        jnp.concatenate(left, axis=1),
        jnp.concatenate(right, axis=1),
        (((1,), (1,)), ((), ())),
        precision=lax.Precision.HIGHEST,
        preferred_element_type=jnp.float32,
    )


def partial_sweep(fields, rhs, low_edge, high_edge, tab, a, out, cells, electric, magnetic):
    width = min(BLOCK, cells)
    wide = width + LANES
    lane = lax.broadcasted_iota(jnp.int32, (8, width), 1)
    column = lane % TX
    not_last, not_first = column != TX - 1, column != 0
    row = lax.broadcasted_iota(jnp.int32, (8, width), 0)

    def body(step, carry):
        at = pl.multiple_of(step * width, LANES)
        here = pl.ds(at, width)
        mid = pl.ds(pl.multiple_of(at + LANES, LANES), width)

        def ahead(c, k):
            v = fields[c, k, :, pl.ds(pl.multiple_of(at + LANES, LANES), wide)]
            own = v[:, :width]
            dy = pltpu.roll(v, wide - TX, 1)[:, :width] - own
            dx = jnp.where(not_last, pltpu.roll(v, wide - 1, 1)[:, :width], 0.0) - own
            return own, dy, dx

        def behind(c, k):
            v = fields[c, k, :, pl.ds(at, wide)]
            own = v[:, LANES:]
            dy = own - pltpu.roll(v, TX, 1)[:, LANES:]
            dx = own - jnp.where(not_first, pltpu.roll(v, 1, 1)[:, LANES:], 0.0)
            return own, dy, dx

        if electric:
            cos_t, sin_t, ae = (tab[i, :, here] for i in range(3))
        couple = []
        for k in range(3 if electric else 0):
            low, high = [], []
            for c in range(2):
                v = fields[c, k, :, mid]
                i = c * 3 + k
                first = 0.0 if low_edge is None else low_edge[i : i + 1, here]
                last = 0.0 if high_edge is None else high_edge[i : i + 1, here]
                low.append(jnp.where(row == 0, first, pltpu.roll(v, 1, 0)))
                high.append(jnp.where(row == 7, last, pltpu.roll(v, 7, 0)))
            couple.append(
                (
                    cos_t * (low[0] + high[0]) + sin_t * (high[1] - low[1]),
                    cos_t * (low[1] + high[1]) + sin_t * (low[0] - high[0]),
                )
            )
        for c in range(2):
            s = 1.0 if c == 1 else -1.0
            if magnetic:
                ex, ex_y, _ = ahead(c, 0)
                ey, _, ey_x = ahead(c, 1)
                _, ez_y, ez_x = ahead(c, 2)
                sa = s * a
                out(3, 1 - c, here, sa * (rhs[c, 3, :, here] - ez_y - ey))
                out(4, 1 - c, here, sa * (rhs[c, 4, :, here] + ex + ez_x))
                out(5, 1 - c, here, sa * (rhs[c, 5, :, here] - ey_x + ex_y))
            if electric:
                hx, hx_y, _ = behind(c, 3)
                hy, _, hy_x = behind(c, 4)
                _, hz_y, hz_x = behind(c, 5)
                sae = s * ae
                out(0, 1 - c, here, sae * (rhs[c, 0, :, here] + hz_y - hy) - couple[0][1 - c])
                out(1, 1 - c, here, sae * (rhs[c, 1, :, here] + hx - hz_x) - couple[1][1 - c])
                out(2, 1 - c, here, sae * (rhs[c, 2, :, here] + hy_x - hx_y) - couple[2][1 - c])
        return carry

    lax.fori_loop(0, cells // width, body, 0)


def add_edges(low_edge, high_edge, tab, res, here):
    row = lax.broadcasted_iota(jnp.int32, (8, here.stop - here.start), 0)
    cos_t, sin_t = tab[0, :, here], tab[1, :, here]
    for k in range(3):
        low_re, low_im, high_re, high_im = (
            jnp.where(row == at, edge[i : i + 1, here], 0.0)
            for at, edge, i in ((0, low_edge, k), (0, low_edge, 3 + k), (7, high_edge, k), (7, high_edge, 3 + k))
        )
        res[0, k, :, here] -= cos_t * (low_re + high_re) + sin_t * (high_im - low_im)
        res[1, k, :, here] -= cos_t * (low_im + high_im) + sin_t * (low_re - high_re)


def kernel(
    rhs_hbm, field_hbm, eps_hbm, cells_hbm, profile_hbm, count, amp, phase, out_hbm,
    x, y, rhs, res, p_own, q_own, e_next, h_prev, p_next, q_prev, eps, eps_next, cells, profile,
    tab, low_out, high_out, low_in, high_in,
    last_sem, far_sem, passing, pass_recv, pass_send, local_sem, out_sem, eps_sem, edge_send, edge_recv, down_send, down_recv, up_send, up_recv,
):
    h, p = lax.axis_index("harm"), lax.axis_index("prop")
    nh, np_ = lax.axis_size("harm"), lax.axis_size("prop")
    size = rhs.shape[3]
    chunk = size // CHUNKS
    below, above = {"prop": p - 1}, {"prop": p + 1}
    has_below, has_above = p > 0, p < np_ - 1
    has_low, has_high = h > 0, h < nh - 1

    near_above, near_below = has_above & (p != LAST), has_below & (p != LAST + 1)
    sides = [
        (LAST, LAST + 1, [UP_FIRST] + sorted({by for *_, is_up, by, _ in RELAYED if is_up} - {UP_FIRST})),
        (LAST + 1, LAST, [DOWN_FIRST] + sorted({by for *_, is_up, by, _ in RELAYED if not is_up} - {DOWN_FIRST})),
    ]
    barrier = pltpu.get_barrier_semaphore()
    signal(near_below, barrier, below)
    signal(near_above, barrier, above)
    signal(has_low, barrier, {"harm": h - 1})
    signal(has_high, barrier, {"harm": h + 1})
    neighbours = sum(
        condition.astype(jnp.int32) for condition in (near_below, near_above, has_low, has_high)
    )
    for start, end, (first, *others) in sides:
        greetings = [(first, start), (start, first), (end, first)]
        for other in others:
            greetings += [(other, start), (other, first)]
        for source, target in greetings:
            signal(p == source, barrier, {"prop": target})
            neighbours += (p == target).astype(jnp.int32)

    interior = slice(LANES, LANES + size)
    loads = [
        pltpu.make_async_copy(field_hbm, x.at[:, :, :, interior], local_sem.at[0]),
        pltpu.make_async_copy(rhs_hbm, rhs, local_sem.at[1]),
        pltpu.make_async_copy(eps_hbm, eps, local_sem.at[2]),
        pltpu.make_async_copy(cells_hbm, cells, local_sem.at[3]),
        pltpu.make_async_copy(profile_hbm, profile, local_sem.at[4]),
    ]
    for load in loads:
        load.start()

    def pack_edges(sweep, fields):
        for c in range(2):
            for k in range(3):
                i = c * 3 + k
                low_out[sweep, i : i + 1, :] = fields[c, k, 0:1, interior]
                high_out[sweep, i : i + 1, :] = fields[c, k, 7:8, interior]

    for sweep in range(2):
        low_out[sweep, 6:8, :] = jnp.zeros((2, size), jnp.float32)
        high_out[sweep, 6:8, :] = jnp.zeros((2, size), jnp.float32)
    loads[0].wait()
    pack_edges(0, x)

    @pl.when(jnp.logical_not(has_low))
    def _():
        low_in[...] = jnp.zeros_like(low_in)

    @pl.when(jnp.logical_not(has_high))
    def _():
        high_in[...] = jnp.zeros_like(high_in)

    @pl.when(jnp.logical_not(has_below))
    def _():
        h_prev[...] = jnp.zeros_like(h_prev)
        q_prev[...] = jnp.zeros_like(q_prev)

    @pl.when(jnp.logical_not(has_above))
    def _():
        e_next[...] = jnp.zeros_like(e_next)
        p_next[...] = jnp.zeros_like(p_next)
        eps_next[...] = jnp.ones_like(eps_next)

    pad = jnp.zeros((2, 3, 8, LANES), jnp.float32)
    for fields in (x, y):
        fields[:, 0:3, :, LANES + size :] = pad
        fields[:, 3:6, :, :LANES] = pad

    harmonic = h * 8 + lax.broadcasted_iota(jnp.int32, (8, 1), 0)
    omega = BASE_FREQUENCY + MOD_FREQUENCY * (harmonic - HARMONICS // 2).astype(jnp.float32)
    a = 1.0 / omega
    loads[1].wait()

    def to_first(k, c, here, value):
        if k in (0, 1):
            p_own[c, k, :, here] = value
        elif k in (3, 4):
            q_own[c, k - 3, :, here] = value
        else:
            y[c, k, :, pl.ds(pl.multiple_of(here.start + LANES, LANES), here.size)] = value

    partial_sweep(x, rhs, None, None, tab, a, to_first, size, False, True)
    pl.semaphore_wait(barrier, neighbours)
    for start, end, (first, *others) in sides:
        for one in (start, *others):
            signal(p == first, far_sem, {"prop": one})

    def lanes(c):
        return slice(c * chunk, (c + 1) * chunk)

    def down_parts(sweep, c):
        src = field_hbm.at[:, 0:2, :, lanes(c)] if sweep == 0 else p_own.at[:, :, :, lanes(c)]
        dst = (e_next, p_next)[sweep].at[:, :, :, lanes(c)]
        return src, dst, down_send.at[sweep, c], down_recv.at[sweep, c]

    def down(sweep, c):
        return remote(*down_parts(sweep, c), below)

    def up_parts(sweep, c):
        src = field_hbm.at[:, 3:5, :, lanes(c)] if sweep == 0 else q_own.at[:, :, :, lanes(c)]
        dst = (h_prev, q_prev)[sweep].at[:, :, :, lanes(c)]
        return src, dst, up_send.at[sweep, c], up_recv.at[sweep, c]

    def up(sweep, c):
        return remote(*up_parts(sweep, c), above)

    eps_copy = remote(eps_hbm, eps_next, eps_sem.at[0], eps_sem.at[1], below)

    def to_pass(sweep, c, i, is_up, by):
        src, _, send, _ = (up_parts if is_up else down_parts)(sweep, c)
        return remote(src, passing.at[sweep, i], send, pass_recv.at[sweep, i], {"prop": by})

    def pass_on(sweep, c, i, is_up):
        _, dst, _, recv = (up_parts if is_up else down_parts)(sweep, c)
        end = LAST + 1 if is_up else LAST
        return remote(passing.at[sweep, i], dst, pass_send.at[sweep, i], recv, {"prop": end})

    def start_pass(sweep, upward):
        for at, c, is_up, by, i in RELAYED:
            if at == sweep and is_up == upward:

                @pl.when(p == (LAST if is_up else LAST + 1))
                def _():
                    to_pass(sweep, c, i, is_up, by).start()

    def start_near(sweep, upward):
        for c in range(CHUNKS):

            @pl.when(near_above if upward else near_below)
            def _():
                (up if upward else down)(sweep, c).start()

    def start_far(sweep, upward):
        for c in range(CHUNKS):
            if (UP_WAYS if upward else DOWN_WAYS)[sweep][c] is None:

                @pl.when(p == (LAST if upward else LAST + 1))
                def _():
                    (up if upward else down)(sweep, c).start()

    def pass_all(sweep, by_first):
        for at, c, is_up, by, i in RELAYED:
            if at == sweep and by_first == (by in (UP_FIRST, DOWN_FIRST)):

                @pl.when(p == by)
                def _():
                    to_pass(sweep, c, i, is_up, by).wait_recv()
                    pass_on(sweep, c, i, is_up).start()

    def wait_far(slabs):
        @pl.when(functools.reduce(jnp.logical_or, [p == one for one in slabs]))
        def _():
            pl.semaphore_wait(far_sem, 1)

    def to_low(sweep):
        return remote(
            low_out.at[sweep], high_in.at[sweep], edge_send.at[sweep, 0], edge_recv.at[sweep, 0],
            {"harm": h - 1},
        )

    def to_high(sweep):
        return remote(
            high_out.at[sweep], low_in.at[sweep], edge_send.at[sweep, 1], edge_recv.at[sweep, 1],
            {"harm": h + 1},
        )

    def send_edges(sweep):
        @pl.when(has_low)
        def _():
            to_low(sweep).start()

        @pl.when(has_high)
        def _():
            to_high(sweep).start()

    def wait_edges(sweep):
        @pl.when(has_high)
        def _():
            to_low(sweep).wait_recv()

        @pl.when(has_low)
        def _():
            to_high(sweep).wait_recv()

    send_edges(0)
    for upward in (True, False):
        start_pass(0, upward)
    start_pass(1, True)
    for upward in (True, False):
        start_near(0, upward)
    start_near(1, True)

    @pl.when(near_below)
    def _():
        eps_copy.start()

    for load in loads[2:]:
        load.wait()
    dense = mod_tables(p.astype(jnp.float32), cells[...], profile[...], count, amp, phase)
    for i in range(size // LANES):
        part = slice(i * LANES, (i + 1) * LANES)
        inverse = 1.0 / eps[:, part]
        tab[0, :, part] = jnp.broadcast_to(dense[i : i + 1, :] * inverse, (8, LANES))
        tab[1, :, part] = jnp.broadcast_to(dense[PROFILES + i : PROFILES + i + 1, :] * inverse, (8, LANES))
        tab[2, :, part] = a * inverse

    wait_far((LAST, LAST + 1))
    for upward in (True, False):
        start_far(0, upward)
    start_far(1, True)

    @pl.when(p == LAST + 1)
    def _():
        eps_copy.start()

    pass_all(0, True)
    wait_edges(0)

    partial_sweep(x, rhs, low_in.at[0], high_in.at[0], tab, a, to_first, size, True, False)
    start_pass(1, False)
    start_near(1, False)
    wait_far([one for _, _, (_, *others) in sides for one in others])
    start_far(1, False)
    pass_all(0, False)
    pass_all(1, True)
    pass_all(1, False)

    for c in range(CHUNKS):

        @pl.when(has_above)
        def _():
            down(0, c).wait_recv()

        @pl.when(has_below)
        def _():
            up(0, c).wait_recv()

        part = lanes(c)
        wide = slice(LANES + c * chunk, LANES + (c + 1) * chunk)
        ae = tab[2, :, part]
        for i in range(2):
            s = 1.0 if i == 1 else -1.0
            y[1 - i, 0, :, wide] = p_own[1 - i, 0, :, part] + s * ae * h_prev[i, 1, :, part]
            y[1 - i, 1, :, wide] = p_own[1 - i, 1, :, part] - s * ae * h_prev[i, 0, :, part]
            y[1 - i, 3, :, wide] = q_own[1 - i, 0, :, part] + s * a * e_next[i, 1, :, part]
            y[1 - i, 4, :, wide] = q_own[1 - i, 1, :, part] - s * a * e_next[i, 0, :, part]

    pack_edges(1, y)
    send_edges(1)

    @pl.when(has_above)
    def _():
        eps_copy.wait_recv()

    above_factor = has_above.astype(jnp.float32)
    below_factor = has_below.astype(jnp.float32)

    def to_second(k, c, here, value):
        res[c, k, :, here] = value

    partial_sweep(y, rhs, None, None, tab, a, to_second, size, True, True)
    outs = [
        pltpu.make_async_copy(res.at[:, k], out_hbm.at[:, k], out_sem.at[0, i])
        for i, k in enumerate((5,))
    ]
    for copy in outs:
        copy.start()

    for c in range(CHUNKS):
        part = lanes(c)
        wide = slice(LANES + c * chunk, LANES + (c + 1) * chunk)

        @pl.when(has_above)
        def _():
            down(1, c).wait_recv()

        @pl.when(has_below)
        def _():
            up(1, c).wait_recv()

        ae = tab[2, :, part]
        ae_next = a * (above_factor / eps_next[:, part])
        a_below = a * below_factor
        for i in range(2):
            s = 1.0 if i == 1 else -1.0
            j = 1 - i
            ex = p_next[i, 0, :, part] - s * ae_next * x[j, 4, :, wide]
            ey = p_next[i, 1, :, part] + s * ae_next * x[j, 3, :, wide]
            hx = q_prev[i, 0, :, part] - s * a_below * x[j, 1, :, wide]
            hy = q_prev[i, 1, :, part] + s * a_below * x[j, 0, :, wide]
            res[j, 0, :, part] += s * ae * hy
            res[j, 1, :, part] -= s * ae * hx
            res[j, 3, :, part] += s * a * ey
            res[j, 4, :, part] -= s * a * ex
        for i, k in enumerate((3,)):
            copy = pltpu.make_async_copy(
                res.at[:, k : k + 2, :, part], out_hbm.at[:, k : k + 2, :, part], out_sem.at[c + 1, i]
            )
            copy.start()
            outs.append(copy)

    wait_edges(1)
    block = min(BLOCK, size)
    for i in range(size // block):
        part = slice(i * block, (i + 1) * block)
        add_edges(low_in.at[1], high_in.at[1], tab, res, part)
        copy = pltpu.make_async_copy(
            res.at[:, 0:3, :, part], out_hbm.at[:, 0:3, :, part], last_sem.at[i]
        )
        copy.start()
        outs.append(copy)

    @pl.when(has_below)
    def _():
        eps_copy.wait_send()

    for sweep in range(2):

        @pl.when(has_low)
        def _():
            to_low(sweep).wait_send()

        @pl.when(has_high)
        def _():
            to_high(sweep).wait_send()

        for c in range(CHUNKS):

            @pl.when(has_below)
            def _():
                down(sweep, c).wait_send()

            @pl.when(has_above)
            def _():
                up(sweep, c).wait_send()

    for sweep, c, is_up, by, i in RELAYED:

        @pl.when(p == by)
        def _():
            pass_on(sweep, c, i, is_up).wait_send()

    for copy in outs:
        copy.wait()


def local(rhs_field, field_guess, permittivity, mod_cells, mod_count, mod_profile, mod_amp, mod_phase):
    size = permittivity.shape[0]
    listed = mod_cells.shape[1]
    f32 = jnp.float32
    whole = (2, 6, 8, size)
    padded = (2, 6, 8, size + 2 * LANES)
    face = (2, 2, 8, size)
    dma = pltpu.SemaphoreType.DMA
    anywhere, smem = pl.BlockSpec(memory_space=pl.ANY), pl.BlockSpec(memory_space=pltpu.SMEM)
    return pl.pallas_call(
        kernel,
        out_shape=jax.ShapeDtypeStruct(whole, f32),
        in_specs=[anywhere] * 5 + [smem] * 3,
        out_specs=anywhere,
        scratch_shapes=[
            pltpu.VMEM(padded, f32), pltpu.VMEM(padded, f32), pltpu.VMEM(whole, f32), pltpu.VMEM(whole, f32),
            *[pltpu.VMEM(face, f32)] * 6,
            pltpu.VMEM((1, size), f32), pltpu.VMEM((1, size), f32),
            pltpu.VMEM((1, listed), jnp.int32), pltpu.VMEM((1, listed), jnp.int32),
            pltpu.VMEM((3, 8, size), f32),
            *[pltpu.VMEM((2, 8, size), f32)] * 4,
            dma((max(1, size // BLOCK),)), pltpu.SemaphoreType.REGULAR, pltpu.VMEM((2, SLOTS, 2, 2, 8, size // CHUNKS), f32), dma((2, SLOTS)), dma((2, SLOTS)),
            dma((5,)), dma((CHUNKS + 1, 2)), dma((2,)), dma((2, 2)), dma((2, 2)),
            *[dma((2, CHUNKS))] * 4,
        ],
        compiler_params=pltpu.CompilerParams(
            collective_id=0, has_side_effects=True, vmem_limit_bytes=60 * 2**20
        ),
        name="sweeps",
    )(rhs_field, field_guess, permittivity.reshape(1, size), mod_cells, mod_profile, mod_count, mod_amp, mod_phase)


def solution(mesh):
    return jax.shard_map(
        local,
        mesh=mesh,
        in_specs=(
            P(None, None, "harm", "prop"),
            P(None, None, "harm", "prop"),
            P("prop"),
            P("prop", None),
            P("prop"),
            P("prop", None),
            P(),
            P(),
        ),
        out_specs=P(None, None, "harm", "prop"),
        check_vma=False,
    )
```

```python
import functools

import jax
import jax.numpy as jnp
from jax import lax
from jax.experimental import pallas as pl
from jax.experimental.pallas import tpu as pltpu
from jax.sharding import PartitionSpec as P

HARMONICS = 64
TX = 64
BASE_FREQUENCY = 6.0
MOD_FREQUENCY = 0.05
WAVE_NUMBER = 0.3
PROFILES = 16
MESH = pl.DeviceIdType.MESH
LANES = 128
BLOCK = 512
CHUNKS = 8
LAST = 15
UP_WAYS = ((0, 12, 3, None, 0, 12, 3, 0), (12, 0, None, 3, 12, None, None, None))
DOWN_WAYS = ((19, 28, 24, None, 19, 28, 24, None), (19, 28, 24, None, 19, 28, None, None))
UP_FIRST, DOWN_FIRST = (0, 19)
RELAYED = [
    (sweep, c, is_up, by, ways[sweep][:c].count(by))
    for is_up, ways in ((True, UP_WAYS), (False, DOWN_WAYS))
    for sweep in range(2)
    for c, by in enumerate(ways[sweep])
    if by is not None
]
SLOTS = 1 + max(i for *_, i in RELAYED)


def remote(src, dst, send, recv, device):
    return pltpu.make_async_remote_copy(
        src_ref=src, dst_ref=dst, send_sem=send, recv_sem=recv, device_id=device, device_id_type=MESH
    )


def signal(condition, sem, device):
    @pl.when(condition)
    def _():
        pl.semaphore_signal(sem, inc=1, device_id=device, device_id_type=MESH)


def mod_tables(plane, cells, profile, count, amp, phase):
    row = lax.broadcasted_iota(jnp.int32, (PROFILES, LANES), 0)
    amps = jnp.zeros((PROFILES, LANES), jnp.float32)
    phases = jnp.zeros((PROFILES, LANES), jnp.float32)
    for i in range(PROFILES):
        amps = jnp.where(row == i, amp[i], amps)
        phases = jnp.where(row == i, phase[i], phases)
    angle = phases - WAVE_NUMBER * plane
    cosines = 0.5 * amps * jnp.cos(angle)
    sines = 0.5 * amps * jnp.sin(angle)
    length = cells.shape[1]
    live = count[0]
    lane = lax.broadcasted_iota(jnp.int32, (1, LANES), 1)
    low_row = lax.broadcasted_iota(jnp.int32, (LANES, LANES), 0)
    left, right = [], []
    for j in range(length // LANES):
        part = slice(j * LANES, (j + 1) * LANES)
        cell, prof = cells[:, part], profile[:, part]
        active = (lane + j * LANES) < live
        here = (row == cell // LANES) & active
        hit = row == prof
        cosine = jnp.sum(jnp.where(hit, cosines, 0.0), axis=0, keepdims=True)
        sine = jnp.sum(jnp.where(hit, sines, 0.0), axis=0, keepdims=True)
        left.append(
            jnp.concatenate([jnp.where(here, cosine, 0.0), jnp.where(here, sine, 0.0)], axis=0)
        )
        right.append((low_row == cell % LANES).astype(jnp.float32))
    return lax.dot_general(
        jnp.concatenate(left, axis=1),
        jnp.concatenate(right, axis=1),
        (((1,), (1,)), ((), ())),
        precision=lax.Precision.HIGHEST,
        preferred_element_type=jnp.float32,
    )


def partial_sweep(fields, rhs, low_edge, high_edge, tab, a, out, cells, electric, magnetic):
    width = min(BLOCK, cells)
    wide = width + LANES
    lane = lax.broadcasted_iota(jnp.int32, (8, width), 1)
    column = lane % TX
    not_last, not_first = column != TX - 1, column != 0
    row = lax.broadcasted_iota(jnp.int32, (8, width), 0)

    def body(step, carry):
        at = pl.multiple_of(step * width, LANES)
        here = pl.ds(at, width)
        mid = pl.ds(pl.multiple_of(at + LANES, LANES), width)

        def ahead(c, k):
            v = fields[c, k, :, pl.ds(pl.multiple_of(at + LANES, LANES), wide)]
            own = v[:, :width]
            dy = pltpu.roll(v, wide - TX, 1)[:, :width] - own
            dx = jnp.where(not_last, pltpu.roll(v, wide - 1, 1)[:, :width], 0.0) - own
            return own, dy, dx

        def behind(c, k):
            v = fields[c, k, :, pl.ds(at, wide)]
            own = v[:, LANES:]
            dy = own - pltpu.roll(v, TX, 1)[:, LANES:]
            dx = own - jnp.where(not_first, pltpu.roll(v, 1, 1)[:, LANES:], 0.0)
            return own, dy, dx

        if electric:
            cos_t, sin_t, ae = (tab[i, :, here] for i in range(3))
        couple = []
        for k in range(3 if electric else 0):
            low, high = [], []
            for c in range(2):
                v = fields[c, k, :, mid]
                i = c * 3 + k
                first = 0.0 if low_edge is None else low_edge[i : i + 1, here]
                last = 0.0 if high_edge is None else high_edge[i : i + 1, here]
                low.append(jnp.where(row == 0, first, pltpu.roll(v, 1, 0)))
                high.append(jnp.where(row == 7, last, pltpu.roll(v, 7, 0)))
            couple.append(
                (
                    cos_t * (low[0] + high[0]) + sin_t * (high[1] - low[1]),
                    cos_t * (low[1] + high[1]) + sin_t * (low[0] - high[0]),
                )
            )
        for c in range(2):
            s = 1.0 if c == 1 else -1.0
            if magnetic:
                ex, ex_y, _ = ahead(c, 0)
                ey, _, ey_x = ahead(c, 1)
                _, ez_y, ez_x = ahead(c, 2)
                sa = s * a
                out(3, 1 - c, here, sa * (rhs[c, 3, :, here] - ez_y - ey))
                out(4, 1 - c, here, sa * (rhs[c, 4, :, here] + ex + ez_x))
                out(5, 1 - c, here, sa * (rhs[c, 5, :, here] - ey_x + ex_y))
            if electric:
                hx, hx_y, _ = behind(c, 3)
                hy, _, hy_x = behind(c, 4)
                _, hz_y, hz_x = behind(c, 5)
                sae = s * ae
                out(0, 1 - c, here, sae * (rhs[c, 0, :, here] + hz_y - hy) - couple[0][1 - c])
                out(1, 1 - c, here, sae * (rhs[c, 1, :, here] + hx - hz_x) - couple[1][1 - c])
                out(2, 1 - c, here, sae * (rhs[c, 2, :, here] + hy_x - hx_y) - couple[2][1 - c])
        return carry

    lax.fori_loop(0, cells // width, body, 0)


def add_edges(low_edge, high_edge, tab, res, here):
    row = lax.broadcasted_iota(jnp.int32, (8, here.stop - here.start), 0)
    cos_t, sin_t = tab[0, :, here], tab[1, :, here]
    for k in range(3):
        low_re, low_im, high_re, high_im = (
            jnp.where(row == at, edge[i : i + 1, here], 0.0)
            for at, edge, i in ((0, low_edge, k), (0, low_edge, 3 + k), (7, high_edge, k), (7, high_edge, 3 + k))
        )
        res[0, k, :, here] -= cos_t * (low_re + high_re) + sin_t * (high_im - low_im)
        res[1, k, :, here] -= cos_t * (low_im + high_im) + sin_t * (low_re - high_re)


def kernel(
    rhs_hbm, field_hbm, eps_hbm, cells_hbm, profile_hbm, count, amp, phase, out_hbm,
    x, y, rhs, res, p_own, q_own, e_next, h_prev, p_next, q_prev, eps, eps_next, cells, profile,
    tab, low_out, high_out, low_in, high_in,
    last_sem, far_sem, passing, pass_recv, pass_send, local_sem, out_sem, eps_sem, edge_send, edge_recv, down_send, down_recv, up_send, up_recv,
):
    h, p = lax.axis_index("harm"), lax.axis_index("prop")
    nh, np_ = lax.axis_size("harm"), lax.axis_size("prop")
    size = rhs.shape[3]
    chunk = size // CHUNKS
    below, above = {"prop": p - 1}, {"prop": p + 1}
    has_below, has_above = p > 0, p < np_ - 1
    has_low, has_high = h > 0, h < nh - 1

    near_above, near_below = has_above & (p != LAST), has_below & (p != LAST + 1)
    sides = [
        (LAST, LAST + 1, [UP_FIRST] + sorted({by for *_, is_up, by, _ in RELAYED if is_up} - {UP_FIRST})),
        (LAST + 1, LAST, [DOWN_FIRST] + sorted({by for *_, is_up, by, _ in RELAYED if not is_up} - {DOWN_FIRST})),
    ]
    barrier = pltpu.get_barrier_semaphore()
    neighbours = sum(
        condition.astype(jnp.int32) for condition in (near_below, near_above, has_low, has_high)
    )
    for start, end, (first, *others) in sides:
        greetings = [(first, start), (start, first), (end, first)]
        for other in others:
            greetings += [(other, start), (other, first)]
        for source, target in greetings:
            signal(p == source, barrier, {"prop": target})
            neighbours += (p == target).astype(jnp.int32)

    signal(near_below, barrier, below)
    signal(near_above, barrier, above)
    signal(has_low, barrier, {"harm": h - 1})
    signal(has_high, barrier, {"harm": h + 1})

    interior = slice(LANES, LANES + size)
    loads = [
        pltpu.make_async_copy(field_hbm, x.at[:, :, :, interior], local_sem.at[0]),
        pltpu.make_async_copy(rhs_hbm, rhs, local_sem.at[1]),
        pltpu.make_async_copy(eps_hbm, eps, local_sem.at[2]),
        pltpu.make_async_copy(cells_hbm, cells, local_sem.at[3]),
        pltpu.make_async_copy(profile_hbm, profile, local_sem.at[4]),
    ]
    for load in loads:
        load.start()

    def pack_edges(sweep, fields):
        for c in range(2):
            for k in range(3):
                i = c * 3 + k
                low_out[sweep, i : i + 1, :] = fields[c, k, 0:1, interior]
                high_out[sweep, i : i + 1, :] = fields[c, k, 7:8, interior]

    for sweep in range(2):
        low_out[sweep, 6:8, :] = jnp.zeros((2, size), jnp.float32)
        high_out[sweep, 6:8, :] = jnp.zeros((2, size), jnp.float32)
    loads[0].wait()
    pack_edges(0, x)

    @pl.when(jnp.logical_not(has_low))
    def _():
        low_in[...] = jnp.zeros_like(low_in)

    @pl.when(jnp.logical_not(has_high))
    def _():
        high_in[...] = jnp.zeros_like(high_in)

    @pl.when(jnp.logical_not(has_below))
    def _():
        h_prev[...] = jnp.zeros_like(h_prev)
        q_prev[...] = jnp.zeros_like(q_prev)

    @pl.when(jnp.logical_not(has_above))
    def _():
        e_next[...] = jnp.zeros_like(e_next)
        p_next[...] = jnp.zeros_like(p_next)
        eps_next[...] = jnp.ones_like(eps_next)

    pad = jnp.zeros((2, 3, 8, LANES), jnp.float32)
    for fields in (x, y):
        fields[:, 0:3, :, LANES + size :] = pad
        fields[:, 3:6, :, :LANES] = pad

    harmonic = h * 8 + lax.broadcasted_iota(jnp.int32, (8, 1), 0)
    omega = BASE_FREQUENCY + MOD_FREQUENCY * (harmonic - HARMONICS // 2).astype(jnp.float32)
    a = 1.0 / omega
    loads[1].wait()

    def to_first(k, c, here, value):
        if k in (0, 1):
            p_own[c, k, :, here] = value
        elif k in (3, 4):
            q_own[c, k - 3, :, here] = value
        else:
            y[c, k, :, pl.ds(pl.multiple_of(here.start + LANES, LANES), here.size)] = value

    partial_sweep(x, rhs, None, None, tab, a, to_first, size, False, True)
    pl.semaphore_wait(barrier, neighbours)
    for start, end, (first, *others) in sides:
        for one in (start, *others):
            signal(p == first, far_sem, {"prop": one})

    def lanes(c):
        return slice(c * chunk, (c + 1) * chunk)

    def down_parts(sweep, c):
        src = field_hbm.at[:, 0:2, :, lanes(c)] if sweep == 0 else p_own.at[:, :, :, lanes(c)]
        dst = (e_next, p_next)[sweep].at[:, :, :, lanes(c)]
        return src, dst, down_send.at[sweep, c], down_recv.at[sweep, c]

    def down(sweep, c):
        return remote(*down_parts(sweep, c), below)

    def up_parts(sweep, c):
        src = field_hbm.at[:, 3:5, :, lanes(c)] if sweep == 0 else q_own.at[:, :, :, lanes(c)]
        dst = (h_prev, q_prev)[sweep].at[:, :, :, lanes(c)]
        return src, dst, up_send.at[sweep, c], up_recv.at[sweep, c]

    def up(sweep, c):
        return remote(*up_parts(sweep, c), above)

    eps_copy = remote(eps_hbm, eps_next, eps_sem.at[0], eps_sem.at[1], below)

    def to_pass(sweep, c, i, is_up, by):
        src, _, send, _ = (up_parts if is_up else down_parts)(sweep, c)
        return remote(src, passing.at[sweep, i], send, pass_recv.at[sweep, i], {"prop": by})

    def pass_on(sweep, c, i, is_up):
        _, dst, _, recv = (up_parts if is_up else down_parts)(sweep, c)
        end = LAST + 1 if is_up else LAST
        return remote(passing.at[sweep, i], dst, pass_send.at[sweep, i], recv, {"prop": end})

    def start_pass(sweep, upward):
        for at, c, is_up, by, i in RELAYED:
            if at == sweep and is_up == upward:

                @pl.when(p == (LAST if is_up else LAST + 1))
                def _():
                    to_pass(sweep, c, i, is_up, by).start()

    def start_near(sweep, upward):
        for c in range(CHUNKS):

            @pl.when(near_above if upward else near_below)
            def _():
                (up if upward else down)(sweep, c).start()

    def start_far(sweep, upward):
        for c in range(CHUNKS):
            if (UP_WAYS if upward else DOWN_WAYS)[sweep][c] is None:

                @pl.when(p == (LAST if upward else LAST + 1))
                def _():
                    (up if upward else down)(sweep, c).start()

    def pass_all(sweep, by_first):
        for at, c, is_up, by, i in RELAYED:
            if at == sweep and by_first == (by in (UP_FIRST, DOWN_FIRST)):

                @pl.when(p == by)
                def _():
                    to_pass(sweep, c, i, is_up, by).wait_recv()
                    pass_on(sweep, c, i, is_up).start()

    def wait_far(slabs):
        @pl.when(functools.reduce(jnp.logical_or, [p == one for one in slabs]))
        def _():
            pl.semaphore_wait(far_sem, 1)

    def to_low(sweep):
        return remote(
            low_out.at[sweep], high_in.at[sweep], edge_send.at[sweep, 0], edge_recv.at[sweep, 0],
            {"harm": h - 1},
        )

    def to_high(sweep):
        return remote(
            high_out.at[sweep], low_in.at[sweep], edge_send.at[sweep, 1], edge_recv.at[sweep, 1],
            {"harm": h + 1},
        )

    def send_edges(sweep):
        @pl.when(has_low)
        def _():
            to_low(sweep).start()

        @pl.when(has_high)
        def _():
            to_high(sweep).start()

    def wait_edges(sweep):
        @pl.when(has_high)
        def _():
            to_low(sweep).wait_recv()

        @pl.when(has_low)
        def _():
            to_high(sweep).wait_recv()

    send_edges(0)
    for upward in (True, False):
        start_pass(0, upward)
    start_pass(1, True)
    for upward in (True, False):
        start_near(0, upward)
    start_near(1, True)

    @pl.when(near_below)
    def _():
        eps_copy.start()

    for load in loads[2:]:
        load.wait()
    dense = mod_tables(p.astype(jnp.float32), cells[...], profile[...], count, amp, phase)
    for i in range(size // LANES):
        part = slice(i * LANES, (i + 1) * LANES)
        inverse = 1.0 / eps[:, part]
        tab[0, :, part] = jnp.broadcast_to(dense[i : i + 1, :] * inverse, (8, LANES))
        tab[1, :, part] = jnp.broadcast_to(dense[PROFILES + i : PROFILES + i + 1, :] * inverse, (8, LANES))
        tab[2, :, part] = a * inverse

    wait_far((LAST, LAST + 1))
    for upward in (True, False):
        start_far(0, upward)
    start_far(1, True)

    @pl.when(p == LAST + 1)
    def _():
        eps_copy.start()

    pass_all(0, True)
    wait_edges(0)

    partial_sweep(x, rhs, low_in.at[0], high_in.at[0], tab, a, to_first, size, True, False)
    start_pass(1, False)
    start_near(1, False)
    wait_far([one for _, _, (_, *others) in sides for one in others])
    start_far(1, False)
    pass_all(0, False)
    pass_all(1, True)
    pass_all(1, False)

    for c in range(CHUNKS):

        @pl.when(has_above)
        def _():
            down(0, c).wait_recv()

        @pl.when(has_below)
        def _():
            up(0, c).wait_recv()

        part = lanes(c)
        wide = slice(LANES + c * chunk, LANES + (c + 1) * chunk)
        ae = tab[2, :, part]
        for i in range(2):
            s = 1.0 if i == 1 else -1.0
            y[1 - i, 0, :, wide] = p_own[1 - i, 0, :, part] + s * ae * h_prev[i, 1, :, part]
            y[1 - i, 1, :, wide] = p_own[1 - i, 1, :, part] - s * ae * h_prev[i, 0, :, part]
            y[1 - i, 3, :, wide] = q_own[1 - i, 0, :, part] + s * a * e_next[i, 1, :, part]
            y[1 - i, 4, :, wide] = q_own[1 - i, 1, :, part] - s * a * e_next[i, 0, :, part]

    pack_edges(1, y)
    send_edges(1)

    @pl.when(has_above)
    def _():
        eps_copy.wait_recv()

    above_factor = has_above.astype(jnp.float32)
    below_factor = has_below.astype(jnp.float32)

    def to_second(k, c, here, value):
        res[c, k, :, here] = value

    partial_sweep(y, rhs, None, None, tab, a, to_second, size, True, True)
    outs = [
        pltpu.make_async_copy(res.at[:, k], out_hbm.at[:, k], out_sem.at[0, i])
        for i, k in enumerate((5,))
    ]
    for copy in outs:
        copy.start()

    for c in range(CHUNKS):
        part = lanes(c)
        wide = slice(LANES + c * chunk, LANES + (c + 1) * chunk)

        @pl.when(has_above)
        def _():
            down(1, c).wait_recv()

        @pl.when(has_below)
        def _():
            up(1, c).wait_recv()

        ae = tab[2, :, part]
        ae_next = a * (above_factor / eps_next[:, part])
        a_below = a * below_factor
        for i in range(2):
            s = 1.0 if i == 1 else -1.0
            j = 1 - i
            ex = p_next[i, 0, :, part] - s * ae_next * x[j, 4, :, wide]
            ey = p_next[i, 1, :, part] + s * ae_next * x[j, 3, :, wide]
            hx = q_prev[i, 0, :, part] - s * a_below * x[j, 1, :, wide]
            hy = q_prev[i, 1, :, part] + s * a_below * x[j, 0, :, wide]
            res[j, 0, :, part] += s * ae * hy
            res[j, 1, :, part] -= s * ae * hx
            res[j, 3, :, part] += s * a * ey
            res[j, 4, :, part] -= s * a * ex
        for i, k in enumerate((3,)):
            copy = pltpu.make_async_copy(
                res.at[:, k : k + 2, :, part], out_hbm.at[:, k : k + 2, :, part], out_sem.at[c + 1, i]
            )
            copy.start()
            outs.append(copy)

    wait_edges(1)
    block = min(BLOCK, size)
    for i in range(size // block):
        part = slice(i * block, (i + 1) * block)
        add_edges(low_in.at[1], high_in.at[1], tab, res, part)
        copy = pltpu.make_async_copy(
            res.at[:, 0:3, :, part], out_hbm.at[:, 0:3, :, part], last_sem.at[i]
        )
        copy.start()
        outs.append(copy)

    @pl.when(has_below)
    def _():
        eps_copy.wait_send()

    for sweep in range(2):

        @pl.when(has_low)
        def _():
            to_low(sweep).wait_send()

        @pl.when(has_high)
        def _():
            to_high(sweep).wait_send()

        for c in range(CHUNKS):

            @pl.when(has_below)
            def _():
                down(sweep, c).wait_send()

            @pl.when(has_above)
            def _():
                up(sweep, c).wait_send()

    for sweep, c, is_up, by, i in RELAYED:

        @pl.when(p == by)
        def _():
            pass_on(sweep, c, i, is_up).wait_send()

    for copy in outs:
        copy.wait()


def local(rhs_field, field_guess, permittivity, mod_cells, mod_count, mod_profile, mod_amp, mod_phase):
    size = permittivity.shape[0]
    listed = mod_cells.shape[1]
    f32 = jnp.float32
    whole = (2, 6, 8, size)
    padded = (2, 6, 8, size + 2 * LANES)
    face = (2, 2, 8, size)
    dma = pltpu.SemaphoreType.DMA
    anywhere, smem = pl.BlockSpec(memory_space=pl.ANY), pl.BlockSpec(memory_space=pltpu.SMEM)
    return pl.pallas_call(
        kernel,
        out_shape=jax.ShapeDtypeStruct(whole, f32),
        in_specs=[anywhere] * 5 + [smem] * 3,
        out_specs=anywhere,
        scratch_shapes=[
            pltpu.VMEM(padded, f32), pltpu.VMEM(padded, f32), pltpu.VMEM(whole, f32), pltpu.VMEM(whole, f32),
            *[pltpu.VMEM(face, f32)] * 6,
            pltpu.VMEM((1, size), f32), pltpu.VMEM((1, size), f32),
            pltpu.VMEM((1, listed), jnp.int32), pltpu.VMEM((1, listed), jnp.int32),
            pltpu.VMEM((3, 8, size), f32),
            *[pltpu.VMEM((2, 8, size), f32)] * 4,
            dma((max(1, size // BLOCK),)), pltpu.SemaphoreType.REGULAR, pltpu.VMEM((2, SLOTS, 2, 2, 8, size // CHUNKS), f32), dma((2, SLOTS)), dma((2, SLOTS)),
            dma((5,)), dma((CHUNKS + 1, 2)), dma((2,)), dma((2, 2)), dma((2, 2)),
            *[dma((2, CHUNKS))] * 4,
        ],
        compiler_params=pltpu.CompilerParams(
            collective_id=0, has_side_effects=True, vmem_limit_bytes=60 * 2**20
        ),
        name="sweeps",
    )(rhs_field, field_guess, permittivity.reshape(1, size), mod_cells, mod_profile, mod_count, mod_amp, mod_phase)


def solution(mesh):
    return jax.shard_map(
        local,
        mesh=mesh,
        in_specs=(
            P(None, None, "harm", "prop"),
            P(None, None, "harm", "prop"),
            P("prop"),
            P("prop", None),
            P("prop"),
            P("prop", None),
            P(),
            P(),
        ),
        out_specs=P(None, None, "harm", "prop"),
        check_vma=False,
    )
```

```python
import functools

import jax
import jax.numpy as jnp
from jax import lax
from jax.experimental import pallas as pl
from jax.experimental.pallas import tpu as pltpu
from jax.sharding import PartitionSpec as P

HARMONICS = 64
TX = 64
BASE_FREQUENCY = 6.0
MOD_FREQUENCY = 0.05
WAVE_NUMBER = 0.3
PROFILES = 16
MESH = pl.DeviceIdType.MESH
LANES = 128
BLOCK = 512
CHUNKS = 8
LAST = 15
UP_WAYS = ((0, 12, 3, None, 0, 12, 3, 0), (12, 0, None, 3, 12, None, None, None))
DOWN_WAYS = ((19, 28, 24, None, 19, 28, 24, None), (19, 28, 24, None, 19, 28, None, None))
UP_FIRST, DOWN_FIRST = (0, 19)
RELAYED = [
    (sweep, c, is_up, by, ways[sweep][:c].count(by))
    for is_up, ways in ((True, UP_WAYS), (False, DOWN_WAYS))
    for sweep in range(2)
    for c, by in enumerate(ways[sweep])
    if by is not None
]
SLOTS = 1 + max(i for *_, i in RELAYED)


def remote(src, dst, send, recv, device):
    return pltpu.make_async_remote_copy(
        src_ref=src, dst_ref=dst, send_sem=send, recv_sem=recv, device_id=device, device_id_type=MESH
    )


def signal(condition, sem, device):
    @pl.when(condition)
    def _():
        pl.semaphore_signal(sem, inc=1, device_id=device, device_id_type=MESH)


def mod_tables(plane, cells, profile, count, amp, phase):
    row = lax.broadcasted_iota(jnp.int32, (PROFILES, LANES), 0)
    amps = jnp.zeros((PROFILES, LANES), jnp.float32)
    phases = jnp.zeros((PROFILES, LANES), jnp.float32)
    for i in range(PROFILES):
        amps = jnp.where(row == i, amp[i], amps)
        phases = jnp.where(row == i, phase[i], phases)
    angle = phases - WAVE_NUMBER * plane
    cosines = 0.5 * amps * jnp.cos(angle)
    sines = 0.5 * amps * jnp.sin(angle)
    length = cells.shape[1]
    live = count[0]
    lane = lax.broadcasted_iota(jnp.int32, (1, LANES), 1)
    low_row = lax.broadcasted_iota(jnp.int32, (LANES, LANES), 0)
    left, right = [], []
    for j in range(length // LANES):
        part = slice(j * LANES, (j + 1) * LANES)
        cell, prof = cells[:, part], profile[:, part]
        active = (lane + j * LANES) < live
        here = (row == cell // LANES) & active
        hit = row == prof
        cosine = jnp.sum(jnp.where(hit, cosines, 0.0), axis=0, keepdims=True)
        sine = jnp.sum(jnp.where(hit, sines, 0.0), axis=0, keepdims=True)
        left.append(
            jnp.concatenate([jnp.where(here, cosine, 0.0), jnp.where(here, sine, 0.0)], axis=0)
        )
        right.append((low_row == cell % LANES).astype(jnp.float32))
    return lax.dot_general(
        jnp.concatenate(left, axis=1),
        jnp.concatenate(right, axis=1),
        (((1,), (1,)), ((), ())),
        precision=lax.Precision.HIGHEST,
        preferred_element_type=jnp.float32,
    )


def partial_sweep(fields, rhs, low_edge, high_edge, tab, a, out, cells, electric, magnetic):
    width = min(BLOCK, cells)
    wide = width + LANES
    lane = lax.broadcasted_iota(jnp.int32, (8, width), 1)
    column = lane % TX
    not_last, not_first = column != TX - 1, column != 0
    row = lax.broadcasted_iota(jnp.int32, (8, width), 0)

    def body(step, carry):
        at = pl.multiple_of(step * width, LANES)
        here = pl.ds(at, width)
        mid = pl.ds(pl.multiple_of(at + LANES, LANES), width)

        def ahead(c, k):
            v = fields[c, k, :, pl.ds(pl.multiple_of(at + LANES, LANES), wide)]
            own = v[:, :width]
            dy = pltpu.roll(v, wide - TX, 1)[:, :width] - own
            dx = jnp.where(not_last, pltpu.roll(v, wide - 1, 1)[:, :width], 0.0) - own
            return own, dy, dx

        def behind(c, k):
            v = fields[c, k, :, pl.ds(at, wide)]
            own = v[:, LANES:]
            dy = own - pltpu.roll(v, TX, 1)[:, LANES:]
            dx = own - jnp.where(not_first, pltpu.roll(v, 1, 1)[:, LANES:], 0.0)
            return own, dy, dx

        if electric:
            cos_t, sin_t, ae = (tab[i, :, here] for i in range(3))
        couple = []
        for k in range(3 if electric else 0):
            low, high = [], []
            for c in range(2):
                v = fields[c, k, :, mid]
                i = c * 3 + k
                first = 0.0 if low_edge is None else low_edge[i : i + 1, here]
                last = 0.0 if high_edge is None else high_edge[i : i + 1, here]
                low.append(jnp.where(row == 0, first, pltpu.roll(v, 1, 0)))
                high.append(jnp.where(row == 7, last, pltpu.roll(v, 7, 0)))
            couple.append(
                (
                    cos_t * (low[0] + high[0]) + sin_t * (high[1] - low[1]),
                    cos_t * (low[1] + high[1]) + sin_t * (low[0] - high[0]),
                )
            )
        for c in range(2):
            s = 1.0 if c == 1 else -1.0
            if magnetic:
                ex, ex_y, _ = ahead(c, 0)
                ey, _, ey_x = ahead(c, 1)
                _, ez_y, ez_x = ahead(c, 2)
                sa = s * a
                out(3, 1 - c, here, sa * (rhs[c, 3, :, here] - ez_y - ey))
                out(4, 1 - c, here, sa * (rhs[c, 4, :, here] + ex + ez_x))
                out(5, 1 - c, here, sa * (rhs[c, 5, :, here] - ey_x + ex_y))
            if electric:
                hx, hx_y, _ = behind(c, 3)
                hy, _, hy_x = behind(c, 4)
                _, hz_y, hz_x = behind(c, 5)
                sae = s * ae
                out(0, 1 - c, here, sae * (rhs[c, 0, :, here] + hz_y - hy) - couple[0][1 - c])
                out(1, 1 - c, here, sae * (rhs[c, 1, :, here] + hx - hz_x) - couple[1][1 - c])
                out(2, 1 - c, here, sae * (rhs[c, 2, :, here] + hy_x - hx_y) - couple[2][1 - c])
        return carry

    lax.fori_loop(0, cells // width, body, 0)


def add_edges(low_edge, high_edge, tab, places, here):
    row = lax.broadcasted_iota(jnp.int32, (8, here.stop - here.start), 0)
    cos_t, sin_t = tab[0, :, here], tab[1, :, here]
    for k in range(3):
        low_re, low_im, high_re, high_im = (
            jnp.where(row == side, edge[i : i + 1, here], 0.0)
            for side, edge, i in ((0, low_edge, k), (0, low_edge, 3 + k), (7, high_edge, k), (7, high_edge, 3 + k))
        )
        res, at, start = places[k]
        there = slice(here.start + start, here.stop + start)
        res[0, at, :, there] -= cos_t * (low_re + high_re) + sin_t * (high_im - low_im)
        res[1, at, :, there] -= cos_t * (low_im + high_im) + sin_t * (low_re - high_re)


def kernel(
    rhs_hbm, field_hbm, eps_hbm, cells_hbm, profile_hbm, count, amp, phase, out_hbm,
    x, y, rhs, res, p_own, q_own, e_next, h_prev, p_next, q_prev, eps, eps_next, cells, profile,
    tab, low_out, high_out, low_in, high_in,
    last_sem, far_sem, passing, pass_recv, pass_send, local_sem, out_sem, eps_sem, edge_send, edge_recv, down_send, down_recv, up_send, up_recv,
):
    h, p = lax.axis_index("harm"), lax.axis_index("prop")
    nh, np_ = lax.axis_size("harm"), lax.axis_size("prop")
    size = rhs.shape[3]
    chunk = size // CHUNKS
    below, above = {"prop": p - 1}, {"prop": p + 1}
    has_below, has_above = p > 0, p < np_ - 1
    has_low, has_high = h > 0, h < nh - 1

    near_above, near_below = has_above & (p != LAST), has_below & (p != LAST + 1)
    sides = [
        (LAST, LAST + 1, [UP_FIRST] + sorted({by for *_, is_up, by, _ in RELAYED if is_up} - {UP_FIRST})),
        (LAST + 1, LAST, [DOWN_FIRST] + sorted({by for *_, is_up, by, _ in RELAYED if not is_up} - {DOWN_FIRST})),
    ]
    barrier = pltpu.get_barrier_semaphore()
    neighbours = sum(
        condition.astype(jnp.int32) for condition in (near_below, near_above, has_low, has_high)
    )
    for start, end, (first, *others) in sides:
        greetings = [(first, start), (start, first), (end, first)]
        for other in others:
            greetings += [(other, start), (other, first)]
        for source, target in greetings:
            signal(p == source, barrier, {"prop": target})
            neighbours += (p == target).astype(jnp.int32)

    signal(near_below, barrier, below)
    signal(near_above, barrier, above)
    signal(has_low, barrier, {"harm": h - 1})
    signal(has_high, barrier, {"harm": h + 1})

    interior = slice(LANES, LANES + size)
    loads = [
        pltpu.make_async_copy(field_hbm, x.at[:, :, :, interior], local_sem.at[0]),
        pltpu.make_async_copy(rhs_hbm, rhs, local_sem.at[1]),
        pltpu.make_async_copy(eps_hbm, eps, local_sem.at[2]),
        pltpu.make_async_copy(cells_hbm, cells, local_sem.at[3]),
        pltpu.make_async_copy(profile_hbm, profile, local_sem.at[4]),
    ]
    for load in loads:
        load.start()

    def pack_edges(sweep, fields):
        for c in range(2):
            for k in range(3):
                i = c * 3 + k
                low_out[sweep, i : i + 1, :] = fields[c, k, 0:1, interior]
                high_out[sweep, i : i + 1, :] = fields[c, k, 7:8, interior]

    for sweep in range(2):
        low_out[sweep, 6:8, :] = jnp.zeros((2, size), jnp.float32)
        high_out[sweep, 6:8, :] = jnp.zeros((2, size), jnp.float32)
    loads[0].wait()
    pack_edges(0, x)

    @pl.when(jnp.logical_not(has_low))
    def _():
        low_in[...] = jnp.zeros_like(low_in)

    @pl.when(jnp.logical_not(has_high))
    def _():
        high_in[...] = jnp.zeros_like(high_in)

    @pl.when(jnp.logical_not(has_below))
    def _():
        h_prev[...] = jnp.zeros_like(h_prev)
        q_prev[...] = jnp.zeros_like(q_prev)

    @pl.when(jnp.logical_not(has_above))
    def _():
        e_next[...] = jnp.zeros_like(e_next)
        p_next[...] = jnp.zeros_like(p_next)
        eps_next[...] = jnp.ones_like(eps_next)

    pad = jnp.zeros((2, 3, 8, LANES), jnp.float32)
    for fields in (x, y):
        fields[:, 0:3, :, LANES + size :] = pad
        fields[:, 3:6, :, :LANES] = pad

    harmonic = h * 8 + lax.broadcasted_iota(jnp.int32, (8, 1), 0)
    omega = BASE_FREQUENCY + MOD_FREQUENCY * (harmonic - HARMONICS // 2).astype(jnp.float32)
    a = 1.0 / omega
    loads[1].wait()

    def to_first(k, c, here, value):
        if k in (0, 1):
            p_own[c, k, :, here] = value
        elif k in (3, 4):
            q_own[c, k - 3, :, here] = value
        else:
            y[c, k, :, pl.ds(pl.multiple_of(here.start + LANES, LANES), here.size)] = value

    partial_sweep(x, rhs, None, None, tab, a, to_first, size, False, True)
    pl.semaphore_wait(barrier, neighbours)
    for start, end, (first, *others) in sides:
        for one in (start, *others):
            signal(p == first, far_sem, {"prop": one})

    def lanes(c):
        return slice(c * chunk, (c + 1) * chunk)

    def down_parts(sweep, c):
        src = field_hbm.at[:, 0:2, :, lanes(c)] if sweep == 0 else p_own.at[:, :, :, lanes(c)]
        dst = (e_next, p_next)[sweep].at[:, :, :, lanes(c)]
        return src, dst, down_send.at[sweep, c], down_recv.at[sweep, c]

    def down(sweep, c):
        return remote(*down_parts(sweep, c), below)

    def up_parts(sweep, c):
        src = field_hbm.at[:, 3:5, :, lanes(c)] if sweep == 0 else q_own.at[:, :, :, lanes(c)]
        dst = (h_prev, q_prev)[sweep].at[:, :, :, lanes(c)]
        return src, dst, up_send.at[sweep, c], up_recv.at[sweep, c]

    def up(sweep, c):
        return remote(*up_parts(sweep, c), above)

    eps_copy = remote(eps_hbm, eps_next, eps_sem.at[0], eps_sem.at[1], below)

    def to_pass(sweep, c, i, is_up, by):
        src, _, send, _ = (up_parts if is_up else down_parts)(sweep, c)
        return remote(src, passing.at[sweep, i], send, pass_recv.at[sweep, i], {"prop": by})

    def pass_on(sweep, c, i, is_up):
        _, dst, _, recv = (up_parts if is_up else down_parts)(sweep, c)
        end = LAST + 1 if is_up else LAST
        return remote(passing.at[sweep, i], dst, pass_send.at[sweep, i], recv, {"prop": end})

    def start_pass(sweep, upward):
        for at, c, is_up, by, i in RELAYED:
            if at == sweep and is_up == upward:

                @pl.when(p == (LAST if is_up else LAST + 1))
                def _():
                    to_pass(sweep, c, i, is_up, by).start()

    def start_near(sweep, upward):
        for c in range(CHUNKS):

            @pl.when(near_above if upward else near_below)
            def _():
                (up if upward else down)(sweep, c).start()

    def start_far(sweep, upward):
        for c in range(CHUNKS):
            if (UP_WAYS if upward else DOWN_WAYS)[sweep][c] is None:

                @pl.when(p == (LAST if upward else LAST + 1))
                def _():
                    (up if upward else down)(sweep, c).start()

    def pass_all(sweep, by_first):
        for at, c, is_up, by, i in RELAYED:
            if at == sweep and by_first == (by in (UP_FIRST, DOWN_FIRST)):

                @pl.when(p == by)
                def _():
                    to_pass(sweep, c, i, is_up, by).wait_recv()
                    pass_on(sweep, c, i, is_up).start()

    def wait_far(slabs):
        @pl.when(functools.reduce(jnp.logical_or, [p == one for one in slabs]))
        def _():
            pl.semaphore_wait(far_sem, 1)

    def to_low(sweep):
        return remote(
            low_out.at[sweep], high_in.at[sweep], edge_send.at[sweep, 0], edge_recv.at[sweep, 0],
            {"harm": h - 1},
        )

    def to_high(sweep):
        return remote(
            high_out.at[sweep], low_in.at[sweep], edge_send.at[sweep, 1], edge_recv.at[sweep, 1],
            {"harm": h + 1},
        )

    def send_edges(sweep):
        @pl.when(has_low)
        def _():
            to_low(sweep).start()

        @pl.when(has_high)
        def _():
            to_high(sweep).start()

    def wait_edges(sweep):
        @pl.when(has_high)
        def _():
            to_low(sweep).wait_recv()

        @pl.when(has_low)
        def _():
            to_high(sweep).wait_recv()

    send_edges(0)
    for upward in (True, False):
        start_pass(0, upward)
    start_pass(1, True)
    for upward in (True, False):
        start_near(0, upward)
    start_near(1, True)

    @pl.when(near_below)
    def _():
        eps_copy.start()

    for load in loads[2:]:
        load.wait()
    dense = mod_tables(p.astype(jnp.float32), cells[...], profile[...], count, amp, phase)
    for i in range(size // LANES):
        part = slice(i * LANES, (i + 1) * LANES)
        inverse = 1.0 / eps[:, part]
        tab[0, :, part] = jnp.broadcast_to(dense[i : i + 1, :] * inverse, (8, LANES))
        tab[1, :, part] = jnp.broadcast_to(dense[PROFILES + i : PROFILES + i + 1, :] * inverse, (8, LANES))
        tab[2, :, part] = a * inverse

    partial_sweep(x, rhs, None, None, tab, a, to_first, size, True, False)
    wait_far((LAST, LAST + 1))
    for upward in (True, False):
        start_far(0, upward)
    start_far(1, True)

    @pl.when(p == LAST + 1)
    def _():
        eps_copy.start()

    pass_all(0, True)
    wait_edges(0)

    places = [(p_own, 0, 0), (p_own, 1, 0), (y, 2, LANES)]
    for i in range(size // min(BLOCK, size)):
        add_edges(low_in.at[0], high_in.at[0], tab, places, slice(i * BLOCK, (i + 1) * BLOCK))
    start_pass(1, False)
    start_near(1, False)
    wait_far([one for _, _, (_, *others) in sides for one in others])
    start_far(1, False)
    pass_all(0, False)
    pass_all(1, True)
    pass_all(1, False)

    for c in range(CHUNKS):

        @pl.when(has_above)
        def _():
            down(0, c).wait_recv()

        @pl.when(has_below)
        def _():
            up(0, c).wait_recv()

        part = lanes(c)
        wide = slice(LANES + c * chunk, LANES + (c + 1) * chunk)
        ae = tab[2, :, part]
        for i in range(2):
            s = 1.0 if i == 1 else -1.0
            y[1 - i, 0, :, wide] = p_own[1 - i, 0, :, part] + s * ae * h_prev[i, 1, :, part]
            y[1 - i, 1, :, wide] = p_own[1 - i, 1, :, part] - s * ae * h_prev[i, 0, :, part]
            y[1 - i, 3, :, wide] = q_own[1 - i, 0, :, part] + s * a * e_next[i, 1, :, part]
            y[1 - i, 4, :, wide] = q_own[1 - i, 1, :, part] - s * a * e_next[i, 0, :, part]

    pack_edges(1, y)
    send_edges(1)

    @pl.when(has_above)
    def _():
        eps_copy.wait_recv()

    above_factor = has_above.astype(jnp.float32)
    below_factor = has_below.astype(jnp.float32)

    def to_second(k, c, here, value):
        res[c, k, :, here] = value

    partial_sweep(y, rhs, None, None, tab, a, to_second, size, True, True)
    outs = [
        pltpu.make_async_copy(res.at[:, k], out_hbm.at[:, k], out_sem.at[0, i])
        for i, k in enumerate((5,))
    ]
    for copy in outs:
        copy.start()

    for c in range(CHUNKS):
        part = lanes(c)
        wide = slice(LANES + c * chunk, LANES + (c + 1) * chunk)

        @pl.when(has_above)
        def _():
            down(1, c).wait_recv()

        @pl.when(has_below)
        def _():
            up(1, c).wait_recv()

        ae = tab[2, :, part]
        ae_next = a * (above_factor / eps_next[:, part])
        a_below = a * below_factor
        for i in range(2):
            s = 1.0 if i == 1 else -1.0
            j = 1 - i
            ex = p_next[i, 0, :, part] - s * ae_next * x[j, 4, :, wide]
            ey = p_next[i, 1, :, part] + s * ae_next * x[j, 3, :, wide]
            hx = q_prev[i, 0, :, part] - s * a_below * x[j, 1, :, wide]
            hy = q_prev[i, 1, :, part] + s * a_below * x[j, 0, :, wide]
            res[j, 0, :, part] += s * ae * hy
            res[j, 1, :, part] -= s * ae * hx
            res[j, 3, :, part] += s * a * ey
            res[j, 4, :, part] -= s * a * ex
        for i, k in enumerate((3,)):
            copy = pltpu.make_async_copy(
                res.at[:, k : k + 2, :, part], out_hbm.at[:, k : k + 2, :, part], out_sem.at[c + 1, i]
            )
            copy.start()
            outs.append(copy)

    wait_edges(1)
    block = min(BLOCK, size)
    for i in range(size // block):
        part = slice(i * block, (i + 1) * block)
        add_edges(low_in.at[1], high_in.at[1], tab, [(res, k, 0) for k in range(3)], part)
        copy = pltpu.make_async_copy(
            res.at[:, 0:3, :, part], out_hbm.at[:, 0:3, :, part], last_sem.at[i]
        )
        copy.start()
        outs.append(copy)

    @pl.when(has_below)
    def _():
        eps_copy.wait_send()

    for sweep in range(2):

        @pl.when(has_low)
        def _():
            to_low(sweep).wait_send()

        @pl.when(has_high)
        def _():
            to_high(sweep).wait_send()

        for c in range(CHUNKS):

            @pl.when(has_below)
            def _():
                down(sweep, c).wait_send()

            @pl.when(has_above)
            def _():
                up(sweep, c).wait_send()

    for sweep, c, is_up, by, i in RELAYED:

        @pl.when(p == by)
        def _():
            pass_on(sweep, c, i, is_up).wait_send()

    for copy in outs:
        copy.wait()


def local(rhs_field, field_guess, permittivity, mod_cells, mod_count, mod_profile, mod_amp, mod_phase):
    size = permittivity.shape[0]
    listed = mod_cells.shape[1]
    f32 = jnp.float32
    whole = (2, 6, 8, size)
    padded = (2, 6, 8, size + 2 * LANES)
    face = (2, 2, 8, size)
    dma = pltpu.SemaphoreType.DMA
    anywhere, smem = pl.BlockSpec(memory_space=pl.ANY), pl.BlockSpec(memory_space=pltpu.SMEM)
    return pl.pallas_call(
        kernel,
        out_shape=jax.ShapeDtypeStruct(whole, f32),
        in_specs=[anywhere] * 5 + [smem] * 3,
        out_specs=anywhere,
        scratch_shapes=[
            pltpu.VMEM(padded, f32), pltpu.VMEM(padded, f32), pltpu.VMEM(whole, f32), pltpu.VMEM(whole, f32),
            *[pltpu.VMEM(face, f32)] * 6,
            pltpu.VMEM((1, size), f32), pltpu.VMEM((1, size), f32),
            pltpu.VMEM((1, listed), jnp.int32), pltpu.VMEM((1, listed), jnp.int32),
            pltpu.VMEM((3, 8, size), f32),
            *[pltpu.VMEM((2, 8, size), f32)] * 4,
            dma((max(1, size // BLOCK),)), pltpu.SemaphoreType.REGULAR, pltpu.VMEM((2, SLOTS, 2, 2, 8, size // CHUNKS), f32), dma((2, SLOTS)), dma((2, SLOTS)),
            dma((5,)), dma((CHUNKS + 1, 2)), dma((2,)), dma((2, 2)), dma((2, 2)),
            *[dma((2, CHUNKS))] * 4,
        ],
        compiler_params=pltpu.CompilerParams(
            collective_id=0, has_side_effects=True, vmem_limit_bytes=60 * 2**20
        ),
        name="sweeps",
    )(rhs_field, field_guess, permittivity.reshape(1, size), mod_cells, mod_profile, mod_count, mod_amp, mod_phase)


def solution(mesh):
    return jax.shard_map(
        local,
        mesh=mesh,
        in_specs=(
            P(None, None, "harm", "prop"),
            P(None, None, "harm", "prop"),
            P("prop"),
            P("prop", None),
            P("prop"),
            P("prop", None),
            P(),
            P(),
        ),
        out_specs=P(None, None, "harm", "prop"),
        check_vma=False,
    )
```
